32 devices in a mesh: dp: 2 (over core), row: 4 (over z), col: 4 (over y, x).
Axes of the slice: x: 2, y: 2, z: 4, core: 2. Of those that a mesh axis runs over, the one named last changes fastest.
Arguments:
- inputs: bfloat16 [1024, 8192], P(('dp', 'row'), 'col'), may hold values from -6 to 6
- w_up: bfloat16 [8192, 16384], P('col', 'row'), may hold values from -0.1875 to 0.1875
- mask_up: int32 [32, 64], replicated, may hold values 0 or 1
- w_down: bfloat16 [16384, 8192], P('row', 'col'), may hold values from -0.125 to 0.125
- mask_down: int32 [64, 32], replicated, may hold values 0 or 1
- threshold: float32 [16384], P('row'), may hold values from 0.4 to 1.6
- cotangent: bfloat16 [1024, 8192], P(('dp', 'row'), 'col'), may hold values from -6 to 6
Outputs:
- output: bfloat16 [1024, 8192], P(('dp', 'row'), 'col')
- input_grad: bfloat16 [1024, 8192], P(('dp', 'row'), 'col')
- up_grad: bfloat16 [8192, 16384], P('col', 'row')
- down_grad: bfloat16 [16384, 8192], P('row', 'col')
The draws below stay inside these ranges and needn't reach their ends.
Inputs may be any that keep to these rules, and one draw needn't show every extreme that they name: `mask_up`: 1 keeps a block, 0 zeroes it. `mask_down`: 1 keeps a block, 0 zeroes it.
All inputs are finite; a program needn't handle non-finite values.
Results may differ from the reference program's by a relative error of at most 0.0049.
Values may be sent and summed in bfloat16 or wider, within the bound.
No kernel may reach another device: no remote copies, remote signals or barrier semaphores. Data moves between devices by JAX's collectives and lax.ppermute only.
A program may use at most 256 MiB of HBM per device.

```python
import math
import jax
import jax.numpy as jnp

D = 8192
FF = 16384
BLOCK = 256
STEPS = 4
ROWS_ALL = 1024


def place_ends(values, stream_key, low, largest):
    spot = [jax.random.randint(jax.random.fold_in(stream_key, axis), (), 0, length) for axis, length in enumerate(values.shape)]
    widest = values.shape.index(max(values.shape))
    neighbour = spot[:widest] + [(spot[widest] + 1) % values.shape[widest]] + spot[widest + 1:]
    return values.at[tuple(spot)].set(low).at[tuple(neighbour)].set(largest)


def steps_of(key, dims, split, smallest, high):
    def one(dim, blocks):
        steps = jax.random.uniform(jax.random.fold_in(jax.random.fold_in(key, 6), dim), (blocks,), jnp.float32, smallest / len(split), high / len(split))
        return jnp.repeat(jnp.exp(steps), dims[dim] // blocks).reshape((-1,) + (1,) * (len(dims) - dim - 1))

    gain = one(*split[0])
    for cut in split[1:]:
        gain = gain * one(*cut)
    return gain


def gaussian(stream_key, dims, scale, most, pieces=(), kind=jnp.bfloat16):
    result = jax.random.normal(stream_key, dims, jnp.float32) * scale
    if len(pieces) > 0:
        result = steps_of(stream_key, dims, pieces, -0.22, 0.18) * result
    return jnp.clip(result, min=-most, max=most).astype(kind)


def setup_inputs(seed: int = 0) -> dict:
    seeds = jax.random.split(jax.random.key(seed), 8)
    return {
        "inputs": gaussian(seeds[0], (ROWS_ALL, D), 1.0, 6.0, ((0, 8), (1, 4))),
        "w_up": gaussian(seeds[1], (D, FF), (D // 8) ** -0.5, 0.1875, ((0, 4), (1, 4))),
        "mask_up": place_ends((jax.random.randint(seeds[2], (D // BLOCK, FF // BLOCK), 0, 8) < 1).astype(jnp.int32), jax.random.fold_in(seeds[2], 1), 0, 1),
        "w_down": gaussian(seeds[3], (FF, D), (FF // 8) ** -0.5, 0.125, ((0, 4), (1, 4))),
        "mask_down": place_ends((jax.random.randint(seeds[4], (FF // BLOCK, D // BLOCK), 0, 8) < 1).astype(jnp.int32), jax.random.fold_in(seeds[4], 1), 0, 1),
        "threshold": jnp.clip(jnp.exp(math.log(1.6) - 1.3862944 * jax.random.uniform(seeds[5], (FF,), jnp.float32) ** steps_of(seeds[5], (FF,), ((0, 4),), -0.2, 0.2)), 0.4, 1.6),
        "cotangent": gaussian(seeds[6], (ROWS_ALL, D), 1.0, 6.0, ((0, 8), (1, 4))),
    }


spike_width = 1.0


def masked(weight, mask):
    rows_b = mask.shape[0]
    cols_b = mask.shape[1]
    shaped = weight.reshape(rows_b, BLOCK, cols_b, BLOCK) * mask.astype(weight.dtype)[:, None, :, None]
    return shaped.reshape(weight.shape)


def spiking(current, theta):
    membrane = jnp.zeros((current.shape[0], current.shape[2]), jnp.float32)
    volts = []
    spikes = []
    for step in range(STEPS):
        volt = membrane + current[:, step]
        spike = jnp.clip((volt - theta) / spike_width + 0.5, 0.0, 1.0)
        membrane = volt - theta * spike
        volts.append(volt)
        spikes.append(spike)
    return jnp.stack(volts, 1), jnp.stack(spikes, 1)


def surrogate_back(grad_hidden, current, volts, spikes, theta):
    carry = jnp.zeros((current.shape[0], current.shape[2]), jnp.float32)
    grads = [None] * STEPS
    for step in range(STEPS - 1, -1, -1):
        offset = 2.0 * (volts[:, step] - theta) / spike_width
        gamma = 1.0 / (spike_width * (1.0 + offset * offset))
        dvolt = carry * (1.0 - theta * gamma) + grad_hidden[:, step] * current[:, step] * gamma
        grads[step] = dvolt + grad_hidden[:, step] * spikes[:, step]
        carry = dvolt
    return jnp.stack(grads, 1)


def reference(inputs, w_up, mask_up, w_down, mask_down, threshold, cotangent):
    up_masked = masked(w_up, mask_up)
    down_masked = masked(w_down, mask_down)
    current = jnp.dot(inputs, up_masked, preferred_element_type=jnp.float32)
    cur3 = current.reshape(-1, STEPS, current.shape[1])
    volts, spikes = spiking(cur3, threshold)
    hidden = (spikes * cur3).astype(jnp.bfloat16).reshape(current.shape)
    output = jnp.dot(hidden, down_masked, preferred_element_type=jnp.float32).astype(jnp.bfloat16)
    down_full = jnp.dot(hidden.T, cotangent, preferred_element_type=jnp.float32)
    down_grad = masked(down_full, mask_down).astype(jnp.bfloat16)
    hidden_grad = jnp.dot(cotangent, down_masked.T, preferred_element_type=jnp.float32)
    current_grad = surrogate_back(hidden_grad.reshape(cur3.shape), cur3, volts, spikes, threshold)
    current_grad = current_grad.astype(jnp.bfloat16).reshape(current.shape)
    up_full = jnp.dot(inputs.T, current_grad, preferred_element_type=jnp.float32)
    up_grad = masked(up_full, mask_up).astype(jnp.bfloat16)
    input_grad = jnp.dot(current_grad, up_masked.T, preferred_element_type=jnp.float32).astype(jnp.bfloat16)
    return output, input_grad, up_grad, down_grad
```

```python
import functools

import jax
import jax.numpy as jnp
from jax import lax
from jax.experimental import pallas as pl
from jax.experimental.pallas import tpu as pltpu
from jax.sharding import PartitionSpec as P

BLOCK = 256
STEPS = 4
QUARTERS = 4
LANES = 128
CURRENT_SCALE = 8.0
VMEM_LIMIT = 56 * 1024 * 1024


spike_width = 1.0

VMEM = pl.BlockSpec(memory_space=pltpu.VMEM)
ANY = pl.BlockSpec(memory_space=pl.ANY)


def params():
    return pltpu.CompilerParams(vmem_limit_bytes=VMEM_LIMIT)


def cost(rows, left, right):
    return pl.CostEstimate(
        flops=rows * left * right // 4,
        bytes_accessed=2 * (rows * left + rows * right + left * right // 8),
        transcendentals=0,
    )


def product(left, right, left_dim, right_dim):
    return lax.dot_general(
        left, right, (((left_dim,), (right_dim,)), ((), ())), preferred_element_type=jnp.float32
    )


def scatter_kernel(
    place,
    mask,
    left,
    weight,
    own,
    keep_a,
    keep_b,
    send_y,
    send_x,
    held,
    acc,
    sems,
    *,
    hidden_first,
):
    rows, depth = left.shape
    _, parts, deep, _, _ = held.shape
    width = own.shape[1] // parts
    half = rows // 2
    here = place[0]

    def spot(r, part):
        return ((here ^ r) * parts + part) * width

    def kept(r, part, k):
        unit = spot(r, part) // BLOCK
        return (mask[unit, k] if hidden_first else mask[k, unit]) != 0

    def copy(r, part, k):
        units = pl.ds(pl.multiple_of(spot(r, part), width), width)
        features = pl.ds(k * BLOCK, BLOCK)
        source = weight.at[units, features] if hidden_first else weight.at[features, units]
        return pltpu.make_async_copy(source, held.at[r, part, k], sems.at[r, part, k])

    order = (3, 1, 2, 0)

    def fetch(part, _, r):
        for k in range(deep):

            @pl.when(kept(r, part, k))
            def _():
                copy(r, part, k).start()

        return 0

    for r in order:
        lax.fori_loop(0, parts, functools.partial(fetch, r=r), 0)

    def compute(part, _, r):
        acc[...] = jnp.zeros_like(acc)
        for k in range(deep):

            @pl.when(kept(r, part, k))
            def _():
                copy(r, part, k).wait()
                acc[...] += product(
                    left[:, k * BLOCK : (k + 1) * BLOCK],
                    held[r, part, k],
                    1,
                    1 if hidden_first else 0,
                )

        columns = pl.ds(pl.multiple_of(part * width, width), width)
        if r == 0:
            own[:, columns] = acc[...]
        elif r == 1:
            keep_a[:, columns] = acc[:half]
            send_x[0, :, columns] = acc[half:].astype(send_x.dtype)
        elif r == 2:
            keep_b[:, columns] = acc[half:]
            send_y[0, :, columns] = acc[:half].astype(send_y.dtype)
        else:
            send_y[1, :, columns] = acc[:half].astype(send_y.dtype)
            send_x[1, :, columns] = acc[half:].astype(send_x.dtype)
        return 0

    for r in order:
        lax.fori_loop(0, parts, functools.partial(compute, r=r), 0)


def scatter_product(place, mask, left, weight, hidden_first, kind, name):
    rows, depth = left.shape
    units = weight.shape[0] if hidden_first else weight.shape[1]
    quarter = units // QUARTERS
    width = min(BLOCK, quarter)
    parts = quarter // width
    deep = depth // BLOCK
    half = rows // 2
    block = (width, BLOCK) if hidden_first else (BLOCK, width)
    return pl.pallas_call(
        functools.partial(scatter_kernel, hidden_first=hidden_first),
        grid_spec=pltpu.PrefetchScalarGridSpec(
            num_scalar_prefetch=2,
            grid=(),
            in_specs=[VMEM, ANY],
            out_specs=[VMEM] * 5,
            scratch_shapes=[
                pltpu.VMEM((QUARTERS, parts, deep) + block, weight.dtype),
                pltpu.VMEM((rows, width), jnp.float32),
                pltpu.SemaphoreType.DMA((QUARTERS, parts, deep)),
            ],
        ),
        out_shape=[
            jax.ShapeDtypeStruct((rows, quarter), jnp.float32),
            jax.ShapeDtypeStruct((half, quarter), jnp.float32),
            jax.ShapeDtypeStruct((half, quarter), jnp.float32),
            jax.ShapeDtypeStruct((2, half, quarter), kind),
            jax.ShapeDtypeStruct((2, half, quarter), kind),
        ],
        compiler_params=params(),
        cost_estimate=cost(rows, depth, units),
        name=name,
    )(place, mask, left, weight)


def collect_kernel(*refs, hidden_first, carried):
    place, mask, mine, over_x, over_y, far_a, far_b = refs[:7]
    at = 7
    came = None
    if carried:
        came = refs[at]
        at += 1
    weight, out, whole, held, acc, sems = refs[at:]
    wide, _, parts, _, _ = held.shape
    rows, quarter = mine.shape
    width = quarter // parts
    half = rows // 2
    here = place[0]

    def spot(r, part):
        return ((here ^ r) * parts + part) * width

    def kept(j, r, part):
        unit = spot(r, part) // BLOCK
        return (mask[unit, j] if hidden_first else mask[j, unit]) != 0

    def copy(j, r, part):
        units = pl.ds(pl.multiple_of(spot(r, part), width), width)
        features = pl.ds(pl.multiple_of(j * BLOCK, BLOCK), BLOCK)
        source = weight.at[units, features] if hidden_first else weight.at[features, units]
        return pltpu.make_async_copy(source, held.at[j, r, part], sems.at[j, r, part])

    def fetch(j, _):
        for r in range(QUARTERS):
            for part in range(parts):

                @pl.when(kept(j, r, part))
                def _():
                    copy(j, r, part).start()

        return 0

    lax.fori_loop(0, wide, fetch, 0)
    whole[0] = mine[...]
    whole[1] = over_x[...]
    whole[2] = over_y[...]
    whole[3, :half] = far_a[...]
    whole[3, half:] = far_b[...]

    def compute(j, _):
        columns = pl.ds(pl.multiple_of(j * BLOCK, BLOCK), BLOCK)
        if carried:
            acc[...] = came[:, columns].astype(jnp.float32)
        else:
            acc[...] = jnp.zeros_like(acc)
        for r in range(QUARTERS):
            for part in range(parts):

                @pl.when(kept(j, r, part))
                def _():
                    copy(j, r, part).wait()
                    acc[...] += product(
                        whole[r, :, part * width : (part + 1) * width],
                        held[j, r, part],
                        1,
                        0 if hidden_first else 1,
                    )

        out[:, columns] = acc[...].astype(out.dtype)
        return 0

    lax.fori_loop(0, wide, compute, 0)


def collect_product(place, mask, pieces, came, weight, hidden_first, out_type, name):
    rows, quarter = pieces[0].shape
    features = weight.shape[1] if hidden_first else weight.shape[0]
    width = min(BLOCK, quarter)
    parts = quarter // width
    wide = features // BLOCK
    block = (width, BLOCK) if hidden_first else (BLOCK, width)
    carried = came is not None
    extra = [came] if carried else []
    return pl.pallas_call(
        functools.partial(collect_kernel, hidden_first=hidden_first, carried=carried),
        grid_spec=pltpu.PrefetchScalarGridSpec(
            num_scalar_prefetch=2,
            grid=(),
            in_specs=[VMEM] * (5 + len(extra)) + [ANY],
            out_specs=[VMEM, VMEM],
            scratch_shapes=[
                pltpu.VMEM((wide, QUARTERS, parts) + block, weight.dtype),
                pltpu.VMEM((rows, BLOCK), jnp.float32),
                pltpu.SemaphoreType.DMA((wide, QUARTERS, parts)),
            ],
        ),
        out_shape=[
            jax.ShapeDtypeStruct((rows, features), out_type),
            jax.ShapeDtypeStruct((QUARTERS, rows, quarter), pieces[0].dtype),
        ],
        compiler_params=params(),
        cost_estimate=cost(rows, QUARTERS * quarter, features),
        name=name,
    )(place, mask, *pieces, *extra, weight)


def gather_rows(sources, held, sems):
    rows = sources[0].shape[-2]
    copies = []
    for i, source in enumerate(sources):
        span = pl.ds(i * rows, rows)
        target = held.at[:, span, :] if len(source.shape) == 3 else held.at[span, :]
        copies.append(pltpu.make_async_copy(source, target, sems.at[i]))
    return copies


def weight_grad_kernel(*refs, count, hidden_first):
    place, mask = refs[:2]
    hidden = refs[2 : 2 + count]
    feature = refs[2 + count : 2 + 2 * count]
    out, held_h, held_f, sems_h, sems_f = refs[2 + 2 * count :]
    quarter = held_h.shape[2]
    width = min(BLOCK, quarter)
    parts = quarter // width
    here = place[0]
    step = pl.program_id(0)

    @pl.when(step == 0)
    def _():
        copies = gather_rows(hidden, held_h, sems_h) + gather_rows(feature, held_f, sems_f)
        for copy in copies:
            copy.start()
        for copy in copies:
            copy.wait()

    if hidden_first:
        r, part = step // parts, step % parts
        unit = (((here ^ r) * parts + part) * width) // BLOCK
        columns = pl.ds(pl.multiple_of(part * width, width), width)
        for j in range(out.shape[1] // BLOCK):
            span = slice(j * BLOCK, (j + 1) * BLOCK)

            @pl.when(mask[unit, j] != 0)
            def _():
                out[:, span] = product(held_h[r, :, columns], held_f[:, span], 0, 0).astype(
                    out.dtype
                )

            @pl.when(mask[unit, j] == 0)
            def _():
                out[:, span] = jnp.zeros((width, BLOCK), out.dtype)

    else:
        columns = pl.ds(pl.multiple_of(step * BLOCK, BLOCK), BLOCK)
        for r in range(QUARTERS):
            for part in range(parts):
                first = ((here ^ r) * parts + part) * width
                unit = first // BLOCK
                span = pl.ds(pl.multiple_of(first, width), width)

                @pl.when(mask[step, unit] != 0)
                def _():
                    out[:, span] = product(
                        held_f[:, columns],
                        held_h[r, :, part * width : (part + 1) * width],
                        0,
                        0,
                    ).astype(out.dtype)

                @pl.when(mask[step, unit] == 0)
                def _():
                    out[:, span] = jnp.zeros((BLOCK, width), out.dtype)


def weight_grad(place, mask, hidden, feature, hidden_first, name):
    count = len(hidden)
    _, rows, quarter = hidden[0].shape
    features = feature[0].shape[1]
    units = QUARTERS * quarter
    width = min(BLOCK, quarter)
    parts = quarter // width
    if hidden_first:
        grid = (QUARTERS * parts,)
        out_shape = (units, features)
        out_spec = pl.BlockSpec(
            (width, features),
            lambda i, place, mask: ((place[0] ^ (i // parts)) * parts + i % parts, 0),
        )
    else:
        grid = (features // BLOCK,)
        out_shape = (features, units)
        out_spec = pl.BlockSpec((BLOCK, units), lambda i, place, mask: (i, 0))
    return pl.pallas_call(
        functools.partial(weight_grad_kernel, count=count, hidden_first=hidden_first),
        grid_spec=pltpu.PrefetchScalarGridSpec(
            num_scalar_prefetch=2,
            grid=grid,
            in_specs=[ANY] * (2 * count),
            out_specs=out_spec,
            scratch_shapes=[
                pltpu.VMEM((QUARTERS, count * rows, quarter), hidden[0].dtype),
                pltpu.VMEM((count * rows, features), feature[0].dtype),
                pltpu.SemaphoreType.DMA((count,)),
                pltpu.SemaphoreType.DMA((count,)),
            ],
        ),
        out_shape=jax.ShapeDtypeStruct(out_shape, hidden[0].dtype),
        compiler_params=params(),
        cost_estimate=cost(count * rows, units, features),
        name=name,
    )(place, mask, *hidden, *feature)


def spiking(current, at, theta, tokens):
    membrane = jnp.zeros((tokens, theta.shape[1]), jnp.float32)
    rows = []
    for step in range(STEPS):
        value = current[at, pl.ds(step, tokens, stride=STEPS), :]
        volt = membrane + value
        spike = jnp.clip((volt - theta) / spike_width + 0.5, 0.0, 1.0)
        membrane = volt - theta * spike
        rows.append((value, volt, spike))
    return rows


def forward_kernel(current, theta, hidden, values, results):
    tokens = current.shape[0] // STEPS
    for i in range(current.shape[1] // LANES):
        columns = slice(i * LANES, (i + 1) * LANES)
        values[i] = current[:, columns]
        for step, (value, _, spike) in enumerate(spiking(values, i, theta[:, columns], tokens)):
            results[i, pl.ds(step, tokens, stride=STEPS), :] = spike * value
        hidden[:, columns] = results[i].astype(hidden.dtype)


def backward_kernel(
    own, near_y, near_x, late_a, late_b, theta, current, current_grad, values, grads, results
):
    rows = own.shape[0]
    tokens = rows // STEPS
    half = rows // 2
    for i in range(own.shape[1] // LANES):
        columns = slice(i * LANES, (i + 1) * LANES)
        limit = theta[:, columns]
        values[i] = current[:, columns]
        for span, near, late in (
            (slice(0, half), near_y, late_a),
            (slice(half, rows), near_x, late_b),
        ):
            grads[i, span] = own[span, columns] + (
                near[0, :, columns].astype(jnp.float32) + late[:, columns].astype(jnp.float32)
            )
        steps = spiking(values, i, limit, tokens)
        carry = jnp.zeros((tokens, LANES), jnp.float32)
        for step in range(STEPS - 1, -1, -1):
            value, volt, spike = steps[step]
            grad = grads[i, pl.ds(step, tokens, stride=STEPS), :]
            offset = 2.0 * (volt - limit) / spike_width
            gamma = 1.0 / (spike_width * (1.0 + offset * offset))
            dvolt = carry * (1.0 - limit * gamma) + grad * value * gamma
            results[i, pl.ds(step, tokens, stride=STEPS), :] = dvolt + grad * spike
            carry = dvolt
        current_grad[:, columns] = results[i].astype(current_grad.dtype)


def forward(current, theta):
    rows, quarter = current.shape
    return pl.pallas_call(
        forward_kernel,
        in_specs=[VMEM] * 2,
        out_specs=VMEM,
        scratch_shapes=[pltpu.VMEM((quarter // LANES, rows, LANES), jnp.float32)] * 2,
        out_shape=jax.ShapeDtypeStruct((rows, quarter), jnp.bfloat16),
        compiler_params=params(),
        name="spiking_forward",
    )(current, theta)


def backward(terms, theta, current):
    rows, quarter = terms[0].shape
    return pl.pallas_call(
        backward_kernel,
        in_specs=[VMEM] * 7,
        out_specs=VMEM,
        scratch_shapes=[pltpu.VMEM((quarter // LANES, rows, LANES), jnp.float32)] * 3,
        out_shape=jax.ShapeDtypeStruct((rows, quarter), jnp.bfloat16),
        compiler_params=params(),
        name="spiking_backward",
    )(*terms, theta, current)


def across(value, flip):
    size = lax.axis_size("col")
    return lax.ppermute(value, "col", [(i, i ^ flip) for i in range(size)])


def other_core(value):
    return lax.ppermute(value, "dp", [(0, 1), (1, 0)])


def around(value):
    size = lax.axis_size("row")
    ring = list(range(0, size, 2)) + list(range(size - 1 - size % 2, 0, -2))
    return lax.ppermute(
        value, "row", [(ring[i], ring[(i + 1) % size]) for i in range(size)]
    )


def reduce_current(pieces):
    own, keep_a, keep_b, send_y, send_x = pieces
    half = own.shape[0] // 2

    def coded(value):
        return (value * CURRENT_SCALE).astype(jnp.float16)

    def decoded(value):
        return value.astype(jnp.float32) * (1.0 / CURRENT_SCALE)

    near_y = across(coded(send_y), 2)
    near_x = across(coded(send_x), 1)
    late_a = across(coded(keep_a + decoded(near_y[1])), 1)
    late_b = across(coded(keep_b + decoded(near_x[1])), 2)
    first = own[:half] + (decoded(near_y[0]) + decoded(late_a))
    second = own[half:] + (decoded(near_x[0]) + decoded(late_b))
    return jnp.concatenate([first, second], axis=0)


def reduce_grad(pieces):
    own, keep_a, keep_b, send_y, send_x = pieces
    near_y = across(send_y, 2)
    near_x = across(send_x, 1)
    late_a = across((keep_a + near_y[1].astype(jnp.float32)).astype(jnp.bfloat16), 1)
    late_b = across((keep_b + near_x[1].astype(jnp.float32)).astype(jnp.bfloat16), 2)
    return own, near_y, near_x, late_a, late_b


def gather_quarters(mine):
    half = mine.shape[0] // 2
    over_x = across(mine, 1)
    over_y = across(mine, 2)
    far_a = across(over_y[:half], 1)
    far_b = across(over_x[half:], 2)
    return mine, over_x, over_y, far_a, far_b


def window(mask, rows_b, cols_b, first_place, second_place):
    return lax.dynamic_slice(
        mask, (first_place * rows_b, second_place * cols_b), (rows_b, cols_b)
    )


def per_device(inputs, w_up, mask_up, w_down, mask_down, threshold, cotangent):
    row_place = lax.axis_index("row")
    col_place = lax.axis_index("col")
    features, units = w_up.shape
    near_up = window(mask_up, features // BLOCK, units // BLOCK, col_place, row_place)
    near_down = window(mask_down, units // BLOCK, features // BLOCK, row_place, col_place)
    place = col_place.astype(jnp.int32).reshape(1)
    quarter = units // QUARTERS
    theta = lax.dynamic_slice(threshold, (col_place * quarter,), (quarter,)).reshape(1, quarter)

    ringed = lax.axis_size("row") <= 4
    if ringed:
        steps = lax.axis_size("row")
        xs, cots = [inputs], [cotangent]
        for _ in range(steps - 1):
            xs.append(around(xs[-1]))
            cots.append(around(cots[-1]))
    else:
        steps = 1
        xs = [lax.all_gather(inputs, "row", axis=0, tiled=True)]
        cots = [lax.all_gather(cotangent, "row", axis=0, tiled=True)]

    out_first = out_came = grad_first = grad_came = None
    hiddens, grads = [], []
    for step in range(steps):
        terms = scatter_product(
            place, near_up, xs[step], w_up, False, jnp.float32, "current_terms"
        )
        grad_terms = scatter_product(
            place, near_down, cots[step], w_down, True, jnp.bfloat16, "hidden_grad_terms"
        )
        current = reduce_current(terms)
        hidden = forward(current, theta)
        hidden_pieces = gather_quarters(hidden)
        current_grad = backward(reduce_grad(grad_terms), theta, current)
        grad_pieces = gather_quarters(current_grad)
        kind = jnp.float32 if step == 0 else jnp.bfloat16
        out_part, hidden_all = collect_product(
            place, near_down, hidden_pieces, out_came, w_down, True, kind, "output_terms"
        )
        grad_part, grad_all = collect_product(
            place, near_up, grad_pieces, grad_came, w_up, False, kind, "input_grad_terms"
        )
        if step == 0:
            out_first, grad_first = out_part, grad_part
        else:
            out_came, grad_came = around(out_part), around(grad_part)
        hiddens.append(hidden_all)
        grads.append(grad_all)

    if ringed and steps > 1:
        output = (out_first + out_came.astype(jnp.float32)).astype(jnp.bfloat16)
        input_grad = (grad_first + grad_came.astype(jnp.float32)).astype(jnp.bfloat16)
    else:
        output = lax.psum_scatter(out_first, "row", scatter_dimension=0, tiled=True)
        input_grad = lax.psum_scatter(grad_first, "row", scatter_dimension=0, tiled=True)
        output, input_grad = output.astype(jnp.bfloat16), input_grad.astype(jnp.bfloat16)

    def both(parts):
        return parts + [other_core(part) for part in parts]

    down_grad = weight_grad(place, near_down, both(hiddens), both(cots), True, "down_grad")
    up_grad = weight_grad(place, near_up, both(grads), both(xs), False, "up_grad")
    return (output, input_grad, up_grad, down_grad)


def solution(mesh):
    in_specs = (
        P(("dp", "row"), "col"),
        P("col", "row"),
        P(),
        P("row", "col"),
        P(),
        P("row"),
        P(("dp", "row"), "col"),
    )
    out_specs = (P(("dp", "row"), "col"), P(("dp", "row"), "col"), P("col", "row"), P("row", "col"))
    return jax.shard_map(
        per_device, mesh=mesh, in_specs=in_specs, out_specs=out_specs, check_vma=False
    )
```

```python
import functools
import math

import jax
import jax.numpy as jnp
from jax import lax
from jax.experimental import pallas as pl
from jax.experimental.pallas import tpu as pltpu
from jax.sharding import PartitionSpec as P

BLOCK = 256
STEPS = 4
QUARTERS = 4
LANES = 128
SLOTS = 32
STAGES = 4
PIECES = 8
CODE_UNIT = 2.0**-13
LARGEST_INPUT = 6.0
LARGEST_WEIGHT = 0.1875
VMEM_LIMIT = 56 * 1024 * 1024


spike_width = 1.0

VMEM = pl.BlockSpec(memory_space=pltpu.VMEM)
SMEM = pl.BlockSpec(memory_space=pltpu.SMEM)
ANY = pl.BlockSpec(memory_space=pl.ANY)


def params():
    return pltpu.CompilerParams(vmem_limit_bytes=VMEM_LIMIT)


def shape(dims, kind):
    return jax.ShapeDtypeStruct(dims, kind)


def product(left, right, left_dim, right_dim):
    return lax.dot_general(
        left, right, (((left_dim,), (right_dim,)), ((), ())), preferred_element_type=jnp.float32
    )


def split_units(units):
    quarter = units // QUARTERS
    width = min(BLOCK, quarter)
    return quarter, width, quarter // width


def code_rate(depth):
    largest = 2.02 * depth * LARGEST_INPUT * LARGEST_WEIGHT
    return 32760.0 / math.log1p(largest / CODE_UNIT)


def encode(value, rate):
    size = jnp.log(1.0 + jnp.abs(value) * (1.0 / CODE_UNIT)) * rate + 0.5
    code = size.astype(jnp.int32)
    return jnp.where(value < 0.0, -code, code).astype(jnp.int16)


def decode(code, rate):
    wide = code.astype(jnp.int32).astype(jnp.float32)
    size = (jnp.exp(jnp.abs(wide) * (1.0 / rate)) - 1.0) * CODE_UNIT
    return jnp.where(wide < 0.0, -size, size)


def lists_kernel(place, mask_up, mask_down, up_list, down_list, *, deep, parts, width):
    col, row = place[0], place[1]
    groups = QUARTERS * parts
    units = groups * width // BLOCK

    def walk(g, counts):
        up, down = counts
        piece = (col ^ (g // parts)) * parts + g % parts
        unit = row * units + piece * width // BLOCK
        for k in range(deep):
            entry = piece * 65536 + g * 256 + k
            feature = col * deep + k
            up_list[up] = entry
            down_list[down] = entry
            up = up + mask_up[feature, unit]
            down = down + mask_down[unit, feature]
        return up, down

    up, down = lax.fori_loop(0, groups, walk, (jnp.int32(0), jnp.int32(0)))
    up_list[groups * deep] = up
    down_list[groups * deep] = down


def kept_lists(place, mask_up, mask_down, features, units):
    _, width, parts = split_units(units)
    deep = features // BLOCK
    size = QUARTERS * parts * deep + 1
    return pl.pallas_call(
        functools.partial(lists_kernel, deep=deep, parts=parts, width=width),
        in_specs=[SMEM] * 3,
        out_specs=[SMEM] * 2,
        out_shape=[shape((size,), jnp.int32)] * 2,
        compiler_params=params(),
        name="kept_blocks",
    )(place, mask_up, mask_down)


def each_kept(lists, weights, held, sems, width, hidden_first, use, meanwhile):
    counts = [entries[entries.shape[0] - 1] for entries in lists]

    def copy(which, entry, slot):
        units = pl.ds(pl.multiple_of((entry >> 16) * width, width), width)
        features = pl.ds(pl.multiple_of((entry & 255) * BLOCK, BLOCK), BLOCK)
        weight = weights[which]
        source = weight.at[units, features] if hidden_first[which] else weight.at[features, units]
        return pltpu.make_async_copy(source, held[which].at[slot], sems.at[which, slot])

    def fetch(base):
        for which in range(2):

            def start(i, _, which=which):
                copy(which, lists[which][base + i], i).start()
                return 0

            lax.fori_loop(0, jnp.clip(counts[which] - base, 0, SLOTS), start, 0)

    fetch(0)
    for slots in held:
        slots[SLOTS] = jnp.zeros(slots.shape[1:], slots.dtype)
    meanwhile()

    def turn(index, _):
        base = index * SLOTS
        live = [jnp.clip(count - base, 0, SLOTS) for count in counts]

        @pl.when(index > 0)
        def _():
            fetch(base)

        for which in range(2):

            def finish(i, _, which=which):
                copy(which, lists[which][base + i], i).wait()
                return 0

            lax.fori_loop(0, live[which], finish, 0)

        def work(i, _):
            for t in range(2):
                spot = i * 2 + t
                for which in range(2):
                    real = spot < live[which]
                    entry = lists[which][jnp.where(real, base + spot, 0)]
                    slot = jnp.where(real, spot, SLOTS)
                    use(which, (entry >> 8) & 255, entry & 255, held[which].at[slot])
            return 0

        lax.fori_loop(0, (jnp.maximum(live[0], live[1]) + 1) // 2, work, 0)
        return 0

    turns = (jnp.maximum(counts[0], counts[1]) + SLOTS - 1) // SLOTS
    lax.fori_loop(0, turns, turn, 0)


def scatter_kernel(
    up_list,
    down_list,
    left,
    w_up,
    w_down,
    own,
    keep_a,
    keep_b,
    send_y,
    send_x,
    turned,
    held_up,
    held_down,
    acc,
    sems,
):
    _, groups, rows, width = acc.shape
    depth = left.shape[2]
    parts = groups // QUARTERS
    half = rows // 2
    rate = code_rate(depth)

    def meanwhile():
        acc[...] = jnp.zeros_like(acc)
        for which in range(2):
            for k in range(depth // BLOCK):
                columns = slice(k * BLOCK, (k + 1) * BLOCK)
                turned[which, columns, :] = left[which, :, columns].T

    def use(which, g, k, block):
        columns = pl.ds(pl.multiple_of(k * BLOCK, BLOCK), BLOCK)
        acc[which, g] += product(left[which, :, columns], block[...], 1, which)

    each_kept(
        (up_list, down_list),
        (w_up, w_down),
        (held_up, held_down),
        sems,
        width,
        (False, True),
        use,
        meanwhile,
    )
    for which in range(2):
        for part in range(parts):
            columns = slice(part * width, (part + 1) * width)
            near_x, near_y, far = (acc.at[which, r * parts + part] for r in (1, 2, 3))
            send_y[which, 0, :, columns] = encode(near_y[:half], rate)
            send_y[which, 1, :, columns] = encode(far[:half], rate)
            send_x[which, 0, :, columns] = encode(near_x[half:], rate)
            send_x[which, 1, :, columns] = encode(far[half:], rate)
            keep_a[which, :, columns] = near_x[:half]
            keep_b[which, :, columns] = near_y[half:]
            own[which, :, columns] = acc[which, part]


def scatter_terms(lists, left, w_up, w_down):
    _, rows, depth = left.shape
    units = w_up.shape[1]
    quarter, width, parts = split_units(units)
    half = rows // 2
    return pl.pallas_call(
        scatter_kernel,
        in_specs=[SMEM, SMEM, VMEM, ANY, ANY],
        out_specs=[VMEM] * 6,
        scratch_shapes=[
            pltpu.VMEM((SLOTS + 1, BLOCK, width), w_up.dtype),
            pltpu.VMEM((SLOTS + 1, width, BLOCK), w_down.dtype),
            pltpu.VMEM((2, QUARTERS * parts, rows, width), jnp.float32),
            pltpu.SemaphoreType.DMA((2, SLOTS)),
        ],
        out_shape=[
            shape((2, rows, quarter), jnp.float32),
            shape((2, half, quarter), jnp.float32),
            shape((2, half, quarter), jnp.float32),
            shape((2, 2, half, quarter), jnp.int16),
            shape((2, 2, half, quarter), jnp.int16),
            shape((2, depth, rows), left.dtype),
        ],
        compiler_params=params(),
        cost_estimate=pl.CostEstimate(
            flops=rows * depth * units // 2, bytes_accessed=16 * 2**20, transcendentals=0
        ),
        name="current_and_hidden_grad_terms",
    )(*lists, left, w_up, w_down)


def relay_kernel(keep_a, keep_b, near_y, near_x, late_a, late_b, *, rate):
    for which in range(2):
        late_a[which] = encode(keep_a[which] + decode(near_y[which, 1], rate), rate)
        late_b[which] = encode(keep_b[which] + decode(near_x[which, 1], rate), rate)


def relay(keep_a, keep_b, near_y, near_x, rate):
    return pl.pallas_call(
        functools.partial(relay_kernel, rate=rate),
        in_specs=[VMEM] * 4,
        out_specs=[VMEM] * 2,
        out_shape=[shape(keep_a.shape, jnp.int16)] * 2,
        compiler_params=params(),
        name="relayed_terms",
    )(keep_a, keep_b, near_y, near_x)


def neuron_kernel(
    own, near_y, near_x, late_a, late_b, theta, both, values, grads, hiddens, results, *, rate
):
    rows = own.shape[1]
    tokens = rows // STEPS
    half = rows // 2
    for i in range(own.shape[2] // LANES):
        columns = slice(i * LANES, (i + 1) * LANES)
        limit = theta[:, columns]
        for which, into in ((0, values), (1, grads)):
            for span, near, late in (
                (slice(0, half), near_y, late_a),
                (slice(half, rows), near_x, late_b),
            ):
                into[i, span] = own[which, span, columns] + (
                    decode(near[which, 0, :, columns], rate)
                    + decode(late[which, :, columns], rate)
                )
        membrane = jnp.zeros((tokens, LANES), jnp.float32)
        steps = []
        for step in range(STEPS):
            value = values[i, pl.ds(step, tokens, stride=STEPS), :]
            volt = membrane + value
            spike = jnp.clip((volt - limit) / spike_width + 0.5, 0.0, 1.0)
            membrane = volt - limit * spike
            hiddens[i, pl.ds(step, tokens, stride=STEPS), :] = spike * value
            steps.append((value, volt, spike))
        both[0, :, columns] = hiddens[i].astype(both.dtype)
        carry = jnp.zeros((tokens, LANES), jnp.float32)
        for step in range(STEPS - 1, -1, -1):
            value, volt, spike = steps[step]
            grad = grads[i, pl.ds(step, tokens, stride=STEPS), :]
            offset = 2.0 * (volt - limit) / spike_width
            gamma = 1.0 / (spike_width * (1.0 + offset * offset))
            dvolt = carry * (1.0 - limit * gamma) + grad * value * gamma
            results[i, pl.ds(step, tokens, stride=STEPS), :] = dvolt + grad * spike
            carry = dvolt
        both[1, :, columns] = results[i].astype(both.dtype)


def neurons(own, near_y, near_x, late_a, late_b, theta, rate):
    _, rows, quarter = own.shape
    return pl.pallas_call(
        functools.partial(neuron_kernel, rate=rate),
        in_specs=[VMEM] * 6,
        out_specs=VMEM,
        scratch_shapes=[pltpu.VMEM((quarter // LANES, rows, LANES), jnp.float32)] * 4,
        out_shape=shape((2, rows, quarter), jnp.bfloat16),
        compiler_params=params(),
        name="spiking_and_surrogate",
    )(own, near_y, near_x, late_a, late_b, theta)


def collect_kernel(*refs, carried):
    up_list, down_list, mine, over_x, over_y, far_a, far_b = refs[:7]
    at = 8 if carried else 7
    w_up, w_down, out, whole, held_up, held_down, acc, sems = refs[at:]
    _, rows, quarter = mine.shape
    wide = acc.shape[1]
    width = held_up.shape[2]
    parts = quarter // width
    half = rows // 2

    def meanwhile():
        whole[:, 0] = mine[...]
        whole[:, 1] = over_x[...]
        whole[:, 2] = over_y[...]
        whole[:, 3, :half] = far_a[...]
        whole[:, 3, half:] = far_b[...]
        if carried:
            came = refs[7]
            first = came.shape[1]
            for which in range(2):
                for j in range(wide):
                    columns = slice(j * BLOCK, (j + 1) * BLOCK)
                    acc[which, j, :first] = came[which, :, columns].astype(jnp.float32)
            if first < rows:
                acc[:, :, first:] = jnp.zeros((2, wide, rows - first, BLOCK), jnp.float32)
        else:
            acc[...] = jnp.zeros_like(acc)

    def use(which, g, k, block):
        r, part = g // parts, g % parts
        columns = pl.ds(pl.multiple_of(part * width, width), width)
        acc[which, k] += product(whole[which, r, :, columns], block[...], 1, which)

    each_kept(
        (down_list, up_list),
        (w_down, w_up),
        (held_down, held_up),
        sems,
        width,
        (True, False),
        use,
        meanwhile,
    )
    for which in range(2):
        for j in range(wide):
            out[which, :, j * BLOCK : (j + 1) * BLOCK] = acc[which, j].astype(out.dtype)


def collect_terms(lists, pieces, came, w_up, w_down, out_type):
    _, rows, quarter = pieces[0].shape
    features, units = w_up.shape
    _, width, _ = split_units(units)
    extra = [] if came is None else [came]
    return pl.pallas_call(
        functools.partial(collect_kernel, carried=came is not None),
        in_specs=[SMEM, SMEM] + [VMEM] * (5 + len(extra)) + [ANY, ANY],
        out_specs=[VMEM, VMEM],
        scratch_shapes=[
            pltpu.VMEM((SLOTS + 1, BLOCK, width), w_up.dtype),
            pltpu.VMEM((SLOTS + 1, width, BLOCK), w_down.dtype),
            pltpu.VMEM((2, features // BLOCK, rows, BLOCK), jnp.float32),
            pltpu.SemaphoreType.DMA((2, SLOTS)),
        ],
        out_shape=[
            shape((2, rows, features), out_type),
            shape((2, QUARTERS, rows, quarter), pieces[0].dtype),
        ],
        compiler_params=params(),
        cost_estimate=pl.CostEstimate(
            flops=rows * features * units // 2, bytes_accessed=16 * 2**20, transcendentals=0
        ),
        name="output_and_input_grad_terms",
    )(*lists, *pieces, *extra, w_up, w_down)


def clear_kernel(place, up, down, rows_up, rows_down, sems):
    rows_up[...] = jnp.zeros_like(rows_up)
    rows_down[...] = jnp.zeros_like(rows_down)
    copies = []
    for which, (whole, rows) in enumerate(((up, rows_up), (down, rows_down))):
        for i in range(PIECES):
            target = whole.at[pl.ds(i * rows.shape[0], rows.shape[0]), :]
            copies.append(pltpu.make_async_copy(rows, target, sems.at[which, i]))
    for copy in copies:
        copy.start()
    for copy in copies:
        copy.wait()


def cleared(place, features, units, kind):
    return pl.pallas_call(
        clear_kernel,
        in_specs=[SMEM],
        out_specs=[ANY, ANY],
        scratch_shapes=[
            pltpu.VMEM((features // PIECES, units), kind),
            pltpu.VMEM((units // PIECES, features), kind),
            pltpu.SemaphoreType.DMA((2, PIECES)),
        ],
        out_shape=[shape((features, units), kind), shape((units, features), kind)],
        compiler_params=params(),
        cost_estimate=pl.CostEstimate(
            flops=0, bytes_accessed=4 * features * units, transcendentals=0
        ),
        name="zero_weight_grads",
    )(place)


def weight_grads_kernel(*refs, count):
    lists = refs[:2]
    units = refs[2 : 2 + count]
    turned = refs[2 + count : 2 + 2 * count]
    outs = refs[4 + 2 * count : 6 + 2 * count]
    held_u, held_f, stage_up, stage_down, load_sems, out_sems = refs[6 + 2 * count :]
    width = stage_up.shape[2]
    parts = held_u.shape[3] // width
    stages = (stage_up, stage_down)

    def loads(which):
        copies = []
        first = 0
        for i in range(count):
            rows = units[i].shape[2]
            span = pl.ds(first, rows)
            first += rows
            copies.append(
                pltpu.make_async_copy(
                    units[i].at[1 - which],
                    held_u.at[1 - which, :, span, :],
                    load_sems.at[which, 0, i],
                )
            )
            copies.append(
                pltpu.make_async_copy(
                    turned[i].at[which], held_f.at[which, :, span], load_sems.at[which, 1, i]
                )
            )
        return copies

    def store(which, n):
        entry = lists[which][n]
        slot = n % STAGES
        piece = pl.ds(pl.multiple_of((entry >> 16) * width, width), width)
        features = pl.ds(pl.multiple_of((entry & 255) * BLOCK, BLOCK), BLOCK)
        out = outs[which]
        target = out.at[piece, features] if which else out.at[features, piece]
        return pltpu.make_async_copy(stages[which].at[slot], target, out_sems.at[which, slot])

    first, second = loads(1), loads(0)
    for copy in first + second:
        copy.start()
    totals = [entries[entries.shape[0] - 1] for entries in lists]
    for which, copies in ((1, first), (0, second)):
        for copy in copies:
            copy.wait()

        def block(n, _, which=which):
            entry = lists[which][n]
            g = (entry >> 8) & 255
            features = pl.ds(pl.multiple_of((entry & 255) * BLOCK, BLOCK), BLOCK)
            columns = pl.ds(pl.multiple_of(g % parts * width, width), width)

            @pl.when(n >= STAGES)
            def _():
                store(which, n - STAGES).wait()

            value = product(
                held_f[which, features, :], held_u[1 - which, g // parts, :, columns], 1, 0
            )
            stage = stages[which]
            stage[n % STAGES] = (value.T if which else value).astype(stage.dtype)
            store(which, n).start()
            return 0

        lax.fori_loop(0, totals[which], block, 0)

    for which in (1, 0):

        def drain(n, _, which=which):
            store(which, n).wait()
            return 0

        lax.fori_loop(jnp.maximum(totals[which] - STAGES, 0), totals[which], drain, 0)


def weight_grads(lists, units, turned, zeros):
    count = len(units)
    quarter = units[0].shape[3]
    rows = sum(piece.shape[2] for piece in units)
    features = turned[0].shape[1]
    width = min(BLOCK, quarter)
    kind = units[0].dtype
    return pl.pallas_call(
        functools.partial(weight_grads_kernel, count=count),
        in_specs=[SMEM] * 2 + [ANY] * (2 * count + 2),
        out_specs=[ANY, ANY],
        scratch_shapes=[
            pltpu.VMEM((2, QUARTERS, rows, quarter), kind),
            pltpu.VMEM((2, features, rows), kind),
            pltpu.VMEM((STAGES, BLOCK, width), kind),
            pltpu.VMEM((STAGES, width, BLOCK), kind),
            pltpu.SemaphoreType.DMA((2, 2, count)),
            pltpu.SemaphoreType.DMA((2, STAGES)),
        ],
        out_shape=[shape(zero.shape, kind) for zero in zeros],
        input_output_aliases={2 + 2 * count: 0, 3 + 2 * count: 1},
        compiler_params=params(),
        cost_estimate=pl.CostEstimate(
            flops=rows * QUARTERS * quarter * features // 2,
            bytes_accessed=32 * 2**20,
            transcendentals=0,
        ),
        name="weight_grads",
    )(*lists, *units, *turned, *zeros)


def after(value, *others):
    return lax.optimization_barrier((value, *others))[0]


def across(value, flip):
    size = lax.axis_size("col")
    return lax.ppermute(value, "col", [(i, i ^ flip) for i in range(size)])


def other_core(value):
    return lax.ppermute(value, "dp", [(0, 1), (1, 0)])


def around(value):
    size = lax.axis_size("row")
    ring = list(range(0, size, 2)) + list(range(size - 1 - size % 2, 0, -2))
    return lax.ppermute(value, "row", [(ring[i], ring[(i + 1) % size]) for i in range(size)])


def per_device(inputs, w_up, mask_up, w_down, mask_down, threshold, cotangent):
    col_place = lax.axis_index("col").astype(jnp.int32)
    row_place = lax.axis_index("row").astype(jnp.int32)
    place = jnp.stack([col_place, row_place])
    features, units = w_up.shape
    quarter = units // QUARTERS
    rate = code_rate(features)
    theta = lax.dynamic_slice(threshold, (col_place * quarter,), (quarter,)).reshape(1, quarter)
    lists = kept_lists(place, mask_up, mask_down, features, units)
    rows = inputs.shape[0]

    ringed = lax.axis_size("row") == 4
    both = jnp.stack([inputs, cotangent])
    if ringed:
        rings = [both, around(both)]
        groups = ((0,), (1,), (2,), (3,))
    else:
        rings = [lax.all_gather(both, "row", axis=1, tiled=True)]
        groups = ((0,),)

    count = len(groups)
    terms, relays, pairs, gathered, wholes = ([None] * count for _ in range(5))
    carry = {"mine": None, "came": None, "last": None, "zeros": None}

    def scatter(i):
        chunk = [rings[j] for j in groups[i]]
        chunk = chunk[0] if len(chunk) == 1 else jnp.concatenate(chunk, axis=1)
        if carry["last"] is not None:
            chunk = after(chunk, carry["last"])
        own, keep_a, keep_b, send_y, send_x, turned = scatter_terms(lists, chunk, w_up, w_down)
        terms[i] = (own, keep_a, keep_b, across(send_y, 2), across(send_x, 1), turned)
        carry["last"] = own

    def hop():
        rings.append(around(after(rings[-1], carry["last"])))

    def clear():
        zeros = cleared(after(place, carry["last"]), features, units, w_up.dtype)
        carry["zeros"] = zeros
        carry["last"] = zeros[0]

    def pass_on(i):
        _, keep_a, keep_b, near_y, near_x, _ = terms[i]
        late_a, late_b = relay(after(keep_a, carry["last"]), keep_b, near_y, near_x, rate)
        relays[i] = (across(late_a, 1), across(late_b, 2))
        carry["last"] = late_a

    def fire(i):
        own, _, _, near_y, near_x, _ = terms[i]
        pair = neurons(after(own, carry["last"]), near_y, near_x, *relays[i], theta, rate)
        half = pair.shape[1] // 2
        over_x = across(pair, 1)
        over_y = across(pair, 2)
        far_a = across(over_y[:, :half], 1)
        far_b = across(over_x[:, half:], 2)
        gathered[i] = (pair, over_x, over_y, far_a, far_b)
        carry["last"] = pair

    def collect(i):
        first = carry["mine"] is None
        kind = jnp.float32 if first else jnp.bfloat16
        pair, *others = gathered[i]
        part, whole = collect_terms(
            lists, (after(pair, carry["last"]), *others), carry["came"], w_up, w_down, kind
        )
        if first:
            carry["mine"] = part
        else:
            came = around(part[:, :rows])
            for j in range(1, len(groups[i])):
                came = around(part[:, j * rows : (j + 1) * rows] + came)
            carry["came"] = came
        wholes[i] = whole
        carry["last"] = whole

    if ringed:
        order = "S0 H R0 S1 H F0 R1 S2 F1 C0 R2 S3 F2 C1 R3 F3 C2 Z C3"
    else:
        order = "S0 R0 F0 Z C0"
    for word in order.split():
        if word == "Z":
            clear()
        elif word == "H":
            hop()
        else:
            {"S": scatter, "R": pass_on, "F": fire, "C": collect}[word[0]](int(word[1]))

    unit_parts = wholes + [other_core(whole) for whole in wholes]
    feature_parts = [term[5] for term in terms] + [other_core(term[5]) for term in terms]
    up_grad, down_grad = weight_grads(lists, unit_parts, feature_parts, carry["zeros"])
    mine, came = after(carry["mine"], up_grad), carry["came"]
    if ringed:
        ends = mine + came.astype(jnp.float32)
    else:
        ends = lax.psum_scatter(mine, "row", scatter_dimension=1, tiled=True)
    output, input_grad = ends[0].astype(jnp.bfloat16), ends[1].astype(jnp.bfloat16)
    return (output, input_grad, up_grad, down_grad)


def solution(mesh):
    in_specs = (
        P(("dp", "row"), "col"),
        P("col", "row"),
        P(),
        P("row", "col"),
        P(),
        P("row"),
        P(("dp", "row"), "col"),
    )
    out_specs = (P(("dp", "row"), "col"), P(("dp", "row"), "col"), P("col", "row"), P("row", "col"))
    return jax.shard_map(
        per_device, mesh=mesh, in_specs=in_specs, out_specs=out_specs, check_vma=False
    )
```

```python
import functools
import math

import jax
import jax.numpy as jnp
from jax import lax
from jax.experimental import pallas as pl
from jax.experimental.pallas import tpu as pltpu
from jax.sharding import PartitionSpec as P

BLOCK = 256
STEPS = 4
QUARTERS = 4
LANES = 128
SLOTS = 32
RELAYS = {}
STAGES = 4
PIECES = 8
CODE_UNIT = 2.0**-13
LARGEST_INPUT = 6.0
LARGEST_WEIGHT = 0.1875
VMEM_LIMIT = 63 * 1024 * 1024 + 768 * 1024


spike_width = 1.0

VMEM = pl.BlockSpec(memory_space=pltpu.VMEM)
SMEM = pl.BlockSpec(memory_space=pltpu.SMEM)
ANY = pl.BlockSpec(memory_space=pl.ANY)


def cost(microseconds):
    return pl.CostEstimate(
        flops=0, bytes_accessed=int(microseconds * 3.69e6), transcendentals=0
    )


def params():
    return pltpu.CompilerParams(vmem_limit_bytes=VMEM_LIMIT)


def shape(dims, kind):
    return jax.ShapeDtypeStruct(dims, kind)


def product(left, right, left_dim, right_dim):
    return lax.dot_general(
        left, right, (((left_dim,), (right_dim,)), ((), ())), preferred_element_type=jnp.float32
    )


def split_units(units):
    quarter = units // QUARTERS
    width = min(BLOCK, quarter)
    return quarter, width, quarter // width


def code_rate(depth):
    largest = 2.02 * depth * LARGEST_INPUT * LARGEST_WEIGHT
    return 32760.0 / math.log1p(largest / CODE_UNIT)


def encode(value, rate):
    size = jnp.log(1.0 + jnp.abs(value) * (1.0 / CODE_UNIT)) * rate + 0.5
    code = size.astype(jnp.int32)
    return jnp.where(value < 0.0, -code, code).astype(jnp.int16)


def decode(code, rate):
    wide = code.astype(jnp.int32).astype(jnp.float32)
    size = (jnp.exp(jnp.abs(wide) * (1.0 / rate)) - 1.0) * CODE_UNIT
    return jnp.where(wide < 0.0, -size, size)


def lists_kernel(place, mask_up, mask_down, up_list, down_list, *, deep, parts, width):
    col, row = place[0], place[1]
    groups = QUARTERS * parts
    units = groups * width // BLOCK

    def walk(g, counts):
        up, down = counts
        piece = (col ^ (g // parts)) * parts + g % parts
        unit = row * units + piece * width // BLOCK
        for k in range(deep):
            entry = piece * 65536 + g * 256 + k
            feature = col * deep + k
            up_list[up] = entry
            down_list[down] = entry
            up = up + mask_up[feature, unit]
            down = down + mask_down[feature, unit]
        return up, down

    up, down = lax.fori_loop(0, groups, walk, (jnp.int32(0), jnp.int32(0)))
    up_list[groups * deep] = up
    down_list[groups * deep] = down


def kept_lists(place, mask_up, mask_down, features, units):
    _, width, parts = split_units(units)
    deep = features // BLOCK
    size = QUARTERS * parts * deep + 1
    return pl.pallas_call(
        functools.partial(lists_kernel, deep=deep, parts=parts, width=width),
        in_specs=[SMEM] * 3,
        out_specs=[SMEM] * 2,
        out_shape=[shape((size,), jnp.int32)] * 2,
        compiler_params=params(),
        cost_estimate=cost(3),
        name="kept_blocks",
    )(place, mask_up, mask_down)


def each_kept(lists, weights, held, sems, width, hidden_first, use, meanwhile):
    kinds = range(len(lists))
    counts = [entries[entries.shape[0] - 1] for entries in lists]
    longest = functools.reduce(jnp.maximum, counts)

    def copy(which, entry, slot):
        units = pl.ds(pl.multiple_of((entry >> 16) * width, width), width)
        features = pl.ds(pl.multiple_of((entry & 255) * BLOCK, BLOCK), BLOCK)
        weight = weights[which]
        source = weight.at[units, features] if hidden_first[which] else weight.at[features, units]
        return pltpu.make_async_copy(source, held[which].at[slot], sems.at[which, slot])

    def fetch(base):
        def start(i, _):
            for which in kinds:

                @pl.when(base + i < counts[which])
                def _():
                    copy(which, lists[which][base + i], i).start()

            return 0

        lax.fori_loop(0, jnp.clip(longest - base, 0, SLOTS), start, 0)

    fetch(0)
    for slots in held:
        slots[SLOTS] = jnp.zeros(slots.shape[1:], slots.dtype)
    meanwhile()

    def turn(index, _):
        base = index * SLOTS
        live = [jnp.clip(count - base, 0, SLOTS) for count in counts]

        @pl.when(index > 0)
        def _():
            fetch(base)

        def work(i, _):
            todo = []
            for t in range(2):
                spot = i * 2 + t
                for which in kinds:
                    real = spot < live[which]
                    entry = lists[which][jnp.where(real, base + spot, 0)]
                    slot = jnp.where(real, spot, SLOTS)

                    @pl.when(real)
                    def _():
                        copy(which, entry, spot).wait()

                    todo.append((which, (entry >> 8) & 255, entry & 255, held[which].at[slot]))
            for item in todo:
                use(*item)
            return 0

        lax.fori_loop(0, (jnp.clip(longest - base, 0, SLOTS) + 1) // 2, work, 0)
        return 0

    lax.fori_loop(0, (longest + SLOTS - 1) // SLOTS, turn, 0)


class Copies:
    def __init__(self, sems):
        self.sems = sems
        self.started = []

    def start(self, source, target):
        copy = pltpu.make_async_copy(source, target, self.sems.at[len(self.started)])
        copy.start()
        self.started.append(copy)
        return copy

    def finish(self):
        for copy in self.started:
            copy.wait()


def scatter_kernel(
    up_list,
    down_list,
    left_x,
    left_c,
    w_up,
    w_down,
    earlier,
    own_out,
    keep_a_out,
    keep_b_out,
    send_y_out,
    send_x_out,
    turned_out,
    left,
    own,
    keep_a,
    keep_b,
    send_y,
    send_x,
    turned,
    held_up,
    held_down,
    acc,
    sems,
    in_sems,
    out_sems,
    *,
    stacked,
    first,
):
    _, groups, rows, width = acc.shape
    depth = left.shape[2]
    parts = groups // QUARTERS
    half = rows // 2
    rate = code_rate(depth)
    out = Copies(out_sems)
    moves = Copies(in_sems)
    for which, source in enumerate((left_x, left_c)):
        moves.start(source.at[which] if stacked else source, left.at[which])

    def meanwhile():
        acc[...] = jnp.zeros_like(acc)
        moves.finish()
        for which in range(2):
            for k in range(depth // BLOCK):
                columns = slice(k * BLOCK, (k + 1) * BLOCK)
                turned[which, columns, :] = left[which, :, columns].T
        out.start(turned, turned_out.at[:, :, pl.ds(first, rows)])

    def use(which, g, k, block):
        columns = pl.ds(pl.multiple_of(k * BLOCK, BLOCK), BLOCK)
        acc[which, g] += product(left[which, :, columns], block[...], 1, which)

    each_kept(
        (up_list, down_list),
        (w_up, w_down),
        (held_up, held_down),
        sems,
        width,
        (False, True),
        use,
        meanwhile,
    )
    for which in range(2):
        for part in range(parts):
            columns = slice(part * width, (part + 1) * width)
            near_x, near_y, far = (acc.at[which, r * parts + part] for r in (1, 2, 3))
            keep_a[which, :, columns] = near_x[:half]
            keep_b[which, :, columns] = near_y[half:]
            own[which, :, columns] = acc[which, part]
            send_y[which, 0, :, columns] = encode(near_y[:half], rate)
            send_y[which, 1, :, columns] = encode(far[:half], rate)
            send_x[which, 0, :, columns] = encode(near_x[half:], rate)
            send_x[which, 1, :, columns] = encode(far[half:], rate)
        for source, target in (
            (keep_a, keep_a_out),
            (keep_b, keep_b_out),
            (own, own_out),
            (send_y, send_y_out),
            (send_x, send_x_out),
        ):
            out.start(source.at[which], target.at[which])
    out.finish()


def scatter_terms(lists, left, w_up, w_down, earlier, first, all_rows):
    stacked = not isinstance(left, tuple)
    kind = left.dtype if stacked else left[0].dtype
    rows, depth = left.shape[1:] if stacked else left[0].shape
    units = w_up.shape[1]
    quarter, width, parts = split_units(units)
    half = rows // 2
    if earlier is None:
        earlier, aliases = w_up, {}
    else:
        aliases = {6: 5}
    outs = [
        ((2, rows, quarter), jnp.float32),
        ((2, half, quarter), jnp.float32),
        ((2, half, quarter), jnp.float32),
        ((2, 2, half, quarter), jnp.int16),
        ((2, 2, half, quarter), jnp.int16),
        ((2, depth, rows), kind),
    ]
    return pl.pallas_call(
        functools.partial(scatter_kernel, stacked=stacked, first=first),
        in_specs=[SMEM, SMEM, ANY, ANY, ANY, ANY, ANY],
        out_specs=[ANY] * 6,
        scratch_shapes=[
            pltpu.VMEM((2, rows, depth), kind),
            *(pltpu.VMEM(*out) for out in outs),
            pltpu.VMEM((SLOTS + 1, BLOCK, width), w_up.dtype),
            pltpu.VMEM((SLOTS + 1, width, BLOCK), w_down.dtype),
            pltpu.VMEM((2, QUARTERS * parts, rows, width), jnp.float32),
            pltpu.SemaphoreType.DMA((2, SLOTS)),
            pltpu.SemaphoreType.DMA((2,)),
            pltpu.SemaphoreType.DMA((11,)),
        ],
        out_shape=[shape(*out) for out in outs[:5]] + [shape((2, depth, all_rows), kind)],
        input_output_aliases=aliases,
        compiler_params=params(),
        cost_estimate=cost(7),
        name="current_and_hidden_grad_terms",
    )(*lists, *((left, left) if stacked else left), w_up, w_down, earlier)


def relay_kernel(keep_a, keep_b, near_y, near_x, late_a, late_b, *, rate):
    for which in range(2):
        late_a[which] = encode(keep_a[which] + decode(near_y[which, 1], rate), rate)
        late_b[which] = encode(keep_b[which] + decode(near_x[which, 1], rate), rate)


def relay(keep_a, keep_b, near_y, near_x, rate):
    return pl.pallas_call(
        functools.partial(relay_kernel, rate=rate),
        in_specs=[VMEM] * 4,
        out_specs=[VMEM] * 2,
        out_shape=[shape(keep_a.shape, jnp.int16)] * 2,
        compiler_params=params(),
        cost_estimate=cost(3),
        name="relayed_terms",
    )(keep_a, keep_b, near_y, near_x)


def neuron_kernel(
    own, near_y, near_x, late_a, late_b, theta, both, values, grads, hiddens, results, *, rate
):
    rows = own.shape[1]
    tokens = rows // STEPS
    half = rows // 2
    for i in range(own.shape[2] // LANES):
        columns = slice(i * LANES, (i + 1) * LANES)
        limit = theta[:, columns]
        for which, into in ((0, values), (1, grads)):
            for span, near, late in (
                (slice(0, half), near_y, late_a),
                (slice(half, rows), near_x, late_b),
            ):
                into[i, span] = own[which, span, columns] + (
                    decode(near[which, 0, :, columns], rate)
                    + decode(late[which, :, columns], rate)
                )
        membrane = jnp.zeros((tokens, LANES), jnp.float32)
        steps = []
        for step in range(STEPS):
            value = values[i, pl.ds(step, tokens, stride=STEPS), :]
            volt = membrane + value
            spike = jnp.clip((volt - limit) / spike_width + 0.5, 0.0, 1.0)
            membrane = volt - limit * spike
            hiddens[i, pl.ds(step, tokens, stride=STEPS), :] = spike * value
            steps.append((value, volt, spike))
        both[0, :, columns] = hiddens[i].astype(both.dtype)
        carry = jnp.zeros((tokens, LANES), jnp.float32)
        for step in range(STEPS - 1, -1, -1):
            value, volt, spike = steps[step]
            grad = grads[i, pl.ds(step, tokens, stride=STEPS), :]
            offset = 2.0 * (volt - limit) / spike_width
            gamma = 1.0 / (spike_width * (1.0 + offset * offset))
            dvolt = carry * (1.0 - limit * gamma) + grad * value * gamma
            results[i, pl.ds(step, tokens, stride=STEPS), :] = dvolt + grad * spike
            carry = dvolt
        both[1, :, columns] = results[i].astype(both.dtype)


def neurons(own, near_y, near_x, late_a, late_b, theta, rate):
    _, rows, quarter = own.shape
    return pl.pallas_call(
        functools.partial(neuron_kernel, rate=rate),
        in_specs=[VMEM] * 6,
        out_specs=VMEM,
        scratch_shapes=[pltpu.VMEM((quarter // LANES, rows, LANES), jnp.float32)] * 4,
        out_shape=shape((2, rows, quarter), jnp.bfloat16),
        compiler_params=params(),
        cost_estimate=cost(4),
        name="spiking_and_surrogate",
    )(own, near_y, near_x, late_a, late_b, theta)


def collect_kernel(*refs, count, carried, first_row):
    refs = list(refs)

    def take(count):
        taken, refs[:count] = refs[:count], []
        return taken

    lists = take(2)
    pieces = take(count)
    came_in = take(1)[0] if carried else None
    weights = take(2)
    _, out, whole_out = take(3)
    held = take(2)
    whole, came, part, acc, sems, in_sems, out_sems = refs
    _, rows, quarter = pieces[0].shape
    wide = acc.shape[1]
    width = min(BLOCK, quarter)
    parts = quarter // width
    moves = Copies(in_sems)
    leave = Copies(out_sems)
    if carried:
        moves.start(came_in, came)
    for r, source in enumerate(pieces[:3]):
        moves.start(source, whole.at[:, r])
    first = 0
    for source in pieces[3:]:
        moves.start(source, whole.at[:, 3, pl.ds(first, source.shape[1])])
        first += source.shape[1]

    def meanwhile():
        moves.finish()
        leave.start(whole, whole_out.at[:, :, pl.ds(first_row, rows), :])
        first = came.shape[1] if carried else 0
        for i in range(2):
            for j in range(wide):
                columns = slice(j * BLOCK, (j + 1) * BLOCK)
                if carried:
                    acc[i, j, :first] = came[i, :, columns].astype(jnp.float32)
                if first < rows:
                    acc[i, j, first:] = jnp.zeros((rows - first, BLOCK), jnp.float32)

    def use(i, g, k, block):
        r, piece = g // parts, g % parts
        columns = pl.ds(pl.multiple_of(piece * width, width), width)
        acc[i, k] += product(whole[i, r, :, columns], block[...], 1, i)

    each_kept(lists, weights, held, sems, width, (True, False), use, meanwhile)
    for i in range(2):
        for j in range(wide):
            part[i, :, j * BLOCK : (j + 1) * BLOCK] = acc[i, j].astype(part.dtype)
        leave.start(part.at[i], out.at[i])
    leave.finish()


def collect_terms(lists, pieces, came, w_up, w_down, out_type, earlier, first, all_rows):
    _, rows, quarter = pieces[0].shape
    features, units = w_up.shape
    _, width, _ = split_units(units)
    extra = [] if came is None else [came]
    came_dims = (2, 16, BLOCK) if came is None else came.shape
    whole_dims = (2, QUARTERS, rows, quarter)
    outs = [
        shape((2, rows, features), out_type),
        shape((2, QUARTERS, all_rows, quarter), pieces[0].dtype),
    ]
    if earlier is None:
        earlier, aliases = w_up, {}
    else:
        aliases = {4 + len(pieces) + len(extra): 1}
    return pl.pallas_call(
        functools.partial(
            collect_kernel, count=len(pieces), carried=came is not None, first_row=first
        ),
        in_specs=[SMEM] * 2 + [ANY] * (3 + len(pieces) + len(extra)),
        out_specs=[ANY] * len(outs),
        scratch_shapes=[
            pltpu.VMEM((SLOTS + 1, width, BLOCK), w_up.dtype),
            pltpu.VMEM((SLOTS + 1, BLOCK, width), w_up.dtype),
            pltpu.VMEM(whole_dims, pieces[0].dtype),
            pltpu.VMEM(came_dims, jnp.bfloat16),
            pltpu.VMEM((2, rows, features), out_type),
            pltpu.VMEM((2, features // BLOCK, rows, BLOCK), jnp.float32),
            pltpu.SemaphoreType.DMA((2, SLOTS)),
            pltpu.SemaphoreType.DMA((6,)),
            pltpu.SemaphoreType.DMA((3,)),
        ],
        out_shape=outs,
        input_output_aliases=aliases,
        compiler_params=params(),
        cost_estimate=cost(7),
        name="output_and_input_grad_terms",
    )(lists[1], lists[0], *pieces, *extra, w_down, w_up, earlier)


def clear_kernel(place, up, down, rows_up, rows_down, sems):
    rows_up[...] = jnp.zeros_like(rows_up)
    rows_down[...] = jnp.zeros_like(rows_down)
    copies = []
    for which, (whole, rows) in enumerate(((up, rows_up), (down, rows_down))):
        for i in range(PIECES):
            target = whole.at[pl.ds(i * rows.shape[0], rows.shape[0]), :]
            copies.append(pltpu.make_async_copy(rows, target, sems.at[which, i]))
    for copy in copies:
        copy.start()
    for copy in copies:
        copy.wait()


def cleared(place, features, units, kind):
    return pl.pallas_call(
        clear_kernel,
        in_specs=[SMEM],
        out_specs=[ANY, ANY],
        scratch_shapes=[
            pltpu.VMEM((features // PIECES, units), kind),
            pltpu.VMEM((units // PIECES, features), kind),
            pltpu.SemaphoreType.DMA((2, PIECES)),
        ],
        out_shape=[shape((features, units), kind), shape((units, features), kind)],
        compiler_params=params(),
        cost_estimate=cost(12),
        name="zero_weight_grads",
    )(place)


def weight_grads_kernel(*refs, places, count):
    lists = refs[:2]
    many = len(places)
    units = refs[2 : 2 + many]
    turned = refs[2 + many : 2 + many + count]
    outs = refs[4 + many + count : 6 + many + count]
    held_u, held_f, stage_up, stage_down, load_sems, out_sems = refs[6 + many + count :]
    width = stage_up.shape[2]
    parts = held_u.shape[3] // width
    stages = (stage_up, stage_down)

    def loads(which):
        pairs = []
        for source, first in zip(units, places):
            span = pl.ds(first, source.shape[2])
            pairs.append((source.at[1 - which], held_u.at[1 - which, :, span, :]))
        first = 0
        for source in turned:
            span = pl.ds(first, source.shape[2])
            first += source.shape[2]
            pairs.append((source.at[which], held_f.at[which, :, span]))
        return [
            pltpu.make_async_copy(source, target, load_sems.at[which, i])
            for i, (source, target) in enumerate(pairs)
        ]

    def store(which, n):
        entry = lists[which][n]
        slot = n % STAGES
        piece = pl.ds(pl.multiple_of((entry >> 16) * width, width), width)
        features = pl.ds(pl.multiple_of((entry & 255) * BLOCK, BLOCK), BLOCK)
        out = outs[which]
        target = out.at[piece, features] if which else out.at[features, piece]
        return pltpu.make_async_copy(stages[which].at[slot], target, out_sems.at[which, slot])

    first, second = loads(1), loads(0)
    for copy in first + second:
        copy.start()
    totals = [entries[entries.shape[0] - 1] for entries in lists]
    for which, copies in ((1, first), (0, second)):
        for copy in copies:
            copy.wait()

        def block(n, _, which=which):
            entry = lists[which][n]
            g = (entry >> 8) & 255
            features = pl.ds(pl.multiple_of((entry & 255) * BLOCK, BLOCK), BLOCK)
            columns = pl.ds(pl.multiple_of(g % parts * width, width), width)

            @pl.when(n >= STAGES)
            def _():
                store(which, n - STAGES).wait()

            value = product(
                held_f[which, features, :], held_u[1 - which, g // parts, :, columns], 1, 0
            )
            stage = stages[which]
            stage[n % STAGES] = (value.T if which else value).astype(stage.dtype)
            store(which, n).start()
            return 0

        lax.fori_loop(0, totals[which], block, 0)

    for which in (1, 0):

        def drain(n, _, which=which):
            store(which, n).wait()
            return 0

        lax.fori_loop(jnp.maximum(totals[which] - STAGES, 0), totals[which], drain, 0)


def weight_grads(lists, units, places, turned, zeros):
    count, many = len(turned), len(units)
    quarter = units[0].shape[-1]
    rows = sum(piece.shape[2] for piece in turned)
    features = turned[0].shape[1]
    width = min(BLOCK, quarter)
    kind = units[0].dtype
    return pl.pallas_call(
        functools.partial(weight_grads_kernel, places=places, count=count),
        in_specs=[SMEM] * 2 + [ANY] * (many + count + 2),
        out_specs=[ANY, ANY],
        scratch_shapes=[
            pltpu.VMEM((2, QUARTERS, rows, quarter), kind),
            pltpu.VMEM((2, features, rows), kind),
            pltpu.VMEM((STAGES, BLOCK, width), kind),
            pltpu.VMEM((STAGES, width, BLOCK), kind),
            pltpu.SemaphoreType.DMA((2, many + count)),
            pltpu.SemaphoreType.DMA((2, STAGES)),
        ],
        out_shape=[shape(zero.shape, kind) for zero in zeros],
        input_output_aliases={2 + many + count: 0, 3 + many + count: 1},
        compiler_params=params(),
        cost_estimate=cost(16),
        name="weight_grads",
    )(*lists, *units, *turned, *zeros)


def after(value, *others):
    return lax.optimization_barrier((value, *others))[0]


def across(value, flip):
    size = lax.axis_size("col")
    return lax.ppermute(value, "col", [(i, i ^ flip) for i in range(size)])


def other_core(value):
    return lax.ppermute(value, "dp", [(0, 1), (1, 0)])


def around(value):
    size = lax.axis_size("row")
    ring = list(range(0, size, 2)) + list(range(size - 1 - size % 2, 0, -2))
    return lax.ppermute(value, "row", [(ring[i], ring[(i + 1) % size]) for i in range(size)])


def per_device(inputs, w_up, mask_up, w_down, mask_down, threshold, cotangent):
    col_place = lax.axis_index("col").astype(jnp.int32)
    row_place = lax.axis_index("row").astype(jnp.int32)
    place = jnp.stack([col_place, row_place])
    features, units = w_up.shape
    quarter = units // QUARTERS
    rate = code_rate(features)
    theta = lax.dynamic_slice(threshold, (col_place * quarter,), (quarter,)).reshape(1, quarter)
    lists = kept_lists(place, mask_up, mask_down.T, features, units)
    rows = inputs.shape[0]

    ringed = lax.axis_size("row") == 4
    if ringed:
        rings = [(inputs, cotangent), around(jnp.stack([inputs, cotangent]))]
        count = 4
    else:
        both = jnp.stack([inputs, cotangent])
        rings = [lax.all_gather(both, "row", axis=1, tiled=True)]
        count = 1
        rows = rings[0].shape[1]

    terms, relays, gathered = ([None] * count for _ in range(3))
    lead = max(count - 1, 1)
    carry = dict.fromkeys(("mine", "came", "last", "zeros", "turned", "whole", "end"))

    def scatter(i):
        chunk = rings[i]
        if carry["last"] is not None:
            chunk = after(chunk, carry["last"])
        own, keep_a, keep_b, send_y, send_x, carry["turned"] = scatter_terms(
            lists, chunk, w_up, w_down, carry["turned"], i * rows, count * rows
        )
        terms[i] = (own, keep_a, keep_b, across(send_y, 2), across(send_x, 1))
        carry["last"] = own

    def hop():
        rings.append(around(after(rings[-1], carry["last"])))

    def clear():
        zeros = cleared(after(place, carry["last"]), features, units, w_up.dtype)
        carry["zeros"] = zeros
        carry["last"] = zeros[0]

    def pass_on(i):
        _, keep_a, keep_b, near_y, near_x = terms[i]
        keep_a = after(keep_a, carry["last"])
        late_a, late_b = relay(keep_a, keep_b, near_y, near_x, rate)
        relays[i] = (across(late_a, 1), across(late_b, 2))
        carry["last"] = late_a

    def fire(i):
        own, _, _, near_y, near_x = terms[i]
        pair = neurons(after(own, carry["last"]), near_y, near_x, *relays[i], theta, rate)
        over_x, over_y = across(pair, 1), across(pair, 2)
        if i in RELAYS:
            far = [across(over_y, 1) if RELAYS[i] == 1 else across(over_x, 2)]
        else:
            half = pair.shape[1] // 2
            far = [across(over_y[:, :half], 1), across(over_x[:, half:], 2)]
        gathered[i] = (pair, over_x, over_y, *far)
        carry["last"] = pair

    def collect(i):
        first = carry["mine"] is None
        kind = jnp.float32 if first else jnp.bfloat16
        pair, *others = gathered[i]
        end = i == lead
        part, whole = collect_terms(
            lists,
            (after(pair, carry["last"]), *others),
            carry["came"],
            w_up,
            w_down,
            kind,
            None if end else carry["whole"],
            0 if end else i * rows,
            rows if end else lead * rows,
        )
        if first:
            carry["mine"] = part
        else:
            carry["came"] = around(part)
        carry["end" if end else "whole"] = whole
        carry["last"] = part

    if ringed:
        order = ("S0", "H", "R0", "S1", "H", "F0", "S2", "R1", "F1", "C0", "R2", "S3", "F2", "C1")
        order += ("R3", "C2", "F3", "Z", "C3")
    else:
        order = ("S0", "R0", "F0", "Z", "C0")
    actions = {"S": scatter, "R": pass_on, "F": fire, "C": collect}
    for word in order:
        if word == "Z":
            clear()
        elif word == "H":
            hop()
        else:
            actions[word[0]](int(word[1]))

    units = [carry["whole"]] + ([carry["end"]] if count > 1 else [])
    units += [other_core(value) for value in units]
    turned = [carry["turned"], other_core(carry["turned"])]
    places, first = [], 0
    for value in units:
        places.append(first)
        first += value.shape[2]
    up_grad, down_grad = weight_grads(lists, units, places, turned, carry["zeros"])
    mine, came = after(carry["mine"], up_grad), carry["came"]
    if ringed:
        ends = [mine[kind] + came[kind].astype(jnp.float32) for kind in range(2)]
    else:
        ends = lax.psum_scatter(mine, "row", scatter_dimension=1, tiled=True)
    output, input_grad = ends[0].astype(jnp.bfloat16), ends[1].astype(jnp.bfloat16)
    return (output, input_grad, up_grad, down_grad)


def solution(mesh):
    in_specs = (
        P(("dp", "row"), "col"),
        P("col", "row"),
        P(),
        P("row", "col"),
        P(),
        P("row"),
        P(("dp", "row"), "col"),
    )
    out_specs = (P(("dp", "row"), "col"), P(("dp", "row"), "col"), P("col", "row"), P("row", "col"))
    return jax.shard_map(
        per_device, mesh=mesh, in_specs=in_specs, out_specs=out_specs, check_vma=False
    )
```

```python
import functools
import math

import jax
import jax.numpy as jnp
from jax import lax
from jax.experimental import pallas as pl
from jax.experimental.pallas import tpu as pltpu
from jax.sharding import PartitionSpec as P

BLOCK = 256
STEPS = 4
QUARTERS = 4
LANES = 128
SLOTS = 32
RELAYS = {}
STAGES = 4
PIECES = 8
CODE_UNIT = 2.0**-13
LARGEST_INPUT = 6.0
LARGEST_WEIGHT = 0.1875
VMEM_LIMIT = 63 * 1024 * 1024 + 768 * 1024


spike_width = 1.0

VMEM = pl.BlockSpec(memory_space=pltpu.VMEM)
SMEM = pl.BlockSpec(memory_space=pltpu.SMEM)
ANY = pl.BlockSpec(memory_space=pl.ANY)


def cost(microseconds):
    return pl.CostEstimate(
        flops=0, bytes_accessed=int(microseconds * 3.69e6), transcendentals=0
    )


def params():
    return pltpu.CompilerParams(vmem_limit_bytes=VMEM_LIMIT)


def shape(dims, kind):
    return jax.ShapeDtypeStruct(dims, kind)


def product(left, right, left_dim, right_dim):
    return lax.dot_general(
        left, right, (((left_dim,), (right_dim,)), ((), ())), preferred_element_type=jnp.float32
    )


def split_units(units):
    quarter = units // QUARTERS
    width = min(BLOCK, quarter)
    return quarter, width, quarter // width


def code_rate(depth):
    largest = 2.02 * depth * LARGEST_INPUT * LARGEST_WEIGHT
    return 32760.0 / math.log1p(largest / CODE_UNIT)


def encode(value, rate):
    size = jnp.log(1.0 + jnp.abs(value) * (1.0 / CODE_UNIT)) * rate + 0.5
    code = size.astype(jnp.int32)
    return jnp.where(value < 0.0, -code, code).astype(jnp.int16)


def decode(code, rate):
    wide = code.astype(jnp.int32).astype(jnp.float32)
    size = (jnp.exp(jnp.abs(wide) * (1.0 / rate)) - 1.0) * CODE_UNIT
    return jnp.where(wide < 0.0, -size, size)


def lists_kernel(place, mask_up, mask_down, up_list, down_list, *, deep, parts, width):
    col, row = place[0], place[1]
    groups = QUARTERS * parts
    units = groups * width // BLOCK

    def walk(g, counts):
        up, down = counts
        piece = (col ^ (g // parts)) * parts + g % parts
        unit = row * units + piece * width // BLOCK
        for k in range(deep):
            entry = piece * 65536 + g * 256 + k
            feature = col * deep + k
            up_list[up] = entry
            down_list[down] = entry
            up = up + mask_up[feature, unit]
            down = down + mask_down[feature, unit]
        return up, down

    up, down = lax.fori_loop(0, groups, walk, (jnp.int32(0), jnp.int32(0)))
    up_list[groups * deep] = up
    down_list[groups * deep] = down


def kept_lists(place, mask_up, mask_down, features, units):
    _, width, parts = split_units(units)
    deep = features // BLOCK
    size = QUARTERS * parts * deep + 1
    return pl.pallas_call(
        functools.partial(lists_kernel, deep=deep, parts=parts, width=width),
        in_specs=[SMEM] * 3,
        out_specs=[SMEM] * 2,
        out_shape=[shape((size,), jnp.int32)] * 2,
        compiler_params=params(),
        cost_estimate=cost(3),
        name="kept_blocks",
    )(place, mask_up, mask_down)


def each_kept(lists, weights, held, sems, width, hidden_first, use, meanwhile):
    kinds = range(len(lists))
    counts = [entries[entries.shape[0] - 1] for entries in lists]
    longest = functools.reduce(jnp.maximum, counts)

    def copy(which, entry, slot):
        units = pl.ds(pl.multiple_of((entry >> 16) * width, width), width)
        features = pl.ds(pl.multiple_of((entry & 255) * BLOCK, BLOCK), BLOCK)
        weight = weights[which]
        source = weight.at[units, features] if hidden_first[which] else weight.at[features, units]
        return pltpu.make_async_copy(source, held[which].at[slot], sems.at[which, slot])

    def fetch(base):
        def start(i, _):
            for which in kinds:

                @pl.when(base + i < counts[which])
                def _():
                    copy(which, lists[which][base + i], i).start()

            return 0

        lax.fori_loop(0, jnp.clip(longest - base, 0, SLOTS), start, 0)

    fetch(0)
    for slots in held:
        slots[SLOTS] = jnp.zeros(slots.shape[1:], slots.dtype)
    meanwhile()

    def turn(index, _):
        base = index * SLOTS
        live = [jnp.clip(count - base, 0, SLOTS) for count in counts]

        @pl.when(index > 0)
        def _():
            fetch(base)

        def work(i, _):
            todo = []
            for t in range(2):
                spot = i * 2 + t
                for which in kinds:
                    real = spot < live[which]
                    entry = lists[which][jnp.where(real, base + spot, 0)]
                    slot = jnp.where(real, spot, SLOTS)

                    @pl.when(real)
                    def _():
                        copy(which, entry, spot).wait()

                    todo.append((which, (entry >> 8) & 255, entry & 255, held[which].at[slot]))
            for item in todo:
                use(*item)
            return 0

        lax.fori_loop(0, (jnp.clip(longest - base, 0, SLOTS) + 1) // 2, work, 0)
        return 0

    lax.fori_loop(0, (longest + SLOTS - 1) // SLOTS, turn, 0)


class Copies:
    def __init__(self, sems):
        self.sems = sems
        self.started = []

    def start(self, source, target):
        copy = pltpu.make_async_copy(source, target, self.sems.at[len(self.started)])
        copy.start()
        self.started.append(copy)
        return copy

    def finish(self):
        for copy in self.started:
            copy.wait()


def scatter_kernel(
    up_list,
    down_list,
    left_x,
    left_c,
    w_up,
    w_down,
    earlier,
    own_out,
    keep_a_out,
    keep_b_out,
    send_y_out,
    send_x_out,
    turned_out,
    left,
    own,
    keep_a,
    keep_b,
    send_y,
    send_x,
    turned,
    held_up,
    held_down,
    acc,
    sems,
    in_sems,
    out_sems,
    *,
    stacked,
    first,
):
    _, groups, rows, width = acc.shape
    depth = left.shape[2]
    parts = groups // QUARTERS
    half = rows // 2
    rate = code_rate(depth)
    out = Copies(out_sems)
    moves = Copies(in_sems)
    for which, source in enumerate((left_x, left_c)):
        moves.start(source.at[which] if stacked else source, left.at[which])

    def meanwhile():
        acc[...] = jnp.zeros_like(acc)
        moves.finish()
        for which in range(2):
            for k in range(depth // BLOCK):
                columns = slice(k * BLOCK, (k + 1) * BLOCK)
                turned[which, columns, :] = left[which, :, columns].T
        out.start(turned, turned_out.at[:, :, pl.ds(first, rows)])

    def use(which, g, k, block):
        columns = pl.ds(pl.multiple_of(k * BLOCK, BLOCK), BLOCK)
        acc[which, g] += product(left[which, :, columns], block[...], 1, which)

    each_kept(
        (up_list, down_list),
        (w_up, w_down),
        (held_up, held_down),
        sems,
        width,
        (False, True),
        use,
        meanwhile,
    )
    for which in range(2):
        for part in range(parts):
            columns = slice(part * width, (part + 1) * width)
            near_x, near_y, far = (acc.at[which, r * parts + part] for r in (1, 2, 3))
            keep_a[which, :, columns] = near_x[:half]
            keep_b[which, :, columns] = near_y[half:]
            own[which, :, columns] = acc[which, part]
            send_y[which, 0, :, columns] = encode(near_y[:half], rate)
            send_y[which, 1, :, columns] = encode(far[:half], rate)
            send_x[which, 0, :, columns] = encode(near_x[half:], rate)
            send_x[which, 1, :, columns] = encode(far[half:], rate)
        for source, target in (
            (keep_a, keep_a_out),
            (keep_b, keep_b_out),
            (own, own_out),
            (send_y, send_y_out),
            (send_x, send_x_out),
        ):
            out.start(source.at[which], target.at[which])
    out.finish()


def scatter_terms(lists, left, w_up, w_down, earlier, first, all_rows):
    stacked = not isinstance(left, tuple)
    kind = left.dtype if stacked else left[0].dtype
    rows, depth = left.shape[1:] if stacked else left[0].shape
    units = w_up.shape[1]
    quarter, width, parts = split_units(units)
    half = rows // 2
    if earlier is None:
        earlier, aliases = w_up, {}
    else:
        aliases = {6: 5}
    outs = [
        ((2, rows, quarter), jnp.float32),
        ((2, half, quarter), jnp.float32),
        ((2, half, quarter), jnp.float32),
        ((2, 2, half, quarter), jnp.int16),
        ((2, 2, half, quarter), jnp.int16),
        ((2, depth, rows), kind),
    ]
    return pl.pallas_call(
        functools.partial(scatter_kernel, stacked=stacked, first=first),
        in_specs=[SMEM, SMEM, ANY, ANY, ANY, ANY, ANY],
        out_specs=[ANY] * 6,
        scratch_shapes=[
            pltpu.VMEM((2, rows, depth), kind),
            *(pltpu.VMEM(*out) for out in outs),
            pltpu.VMEM((SLOTS + 1, BLOCK, width), w_up.dtype),
            pltpu.VMEM((SLOTS + 1, width, BLOCK), w_down.dtype),
            pltpu.VMEM((2, QUARTERS * parts, rows, width), jnp.float32),
            pltpu.SemaphoreType.DMA((2, SLOTS)),
            pltpu.SemaphoreType.DMA((2,)),
            pltpu.SemaphoreType.DMA((11,)),
        ],
        out_shape=[shape(*out) for out in outs[:5]] + [shape((2, depth, all_rows), kind)],
        input_output_aliases=aliases,
        compiler_params=params(),
        cost_estimate=cost(7),
        name="current_and_hidden_grad_terms",
    )(*lists, *((left, left) if stacked else left), w_up, w_down, earlier)


def relay_kernel(keep_a, keep_b, near_y, near_x, late_a, late_b, *, rate):
    for which in range(2):
        late_a[which] = encode(keep_a[which] + decode(near_y[which, 1], rate), rate)
        late_b[which] = encode(keep_b[which] + decode(near_x[which, 1], rate), rate)


def relay(keep_a, keep_b, near_y, near_x, rate):
    return pl.pallas_call(
        functools.partial(relay_kernel, rate=rate),
        in_specs=[VMEM] * 4,
        out_specs=[VMEM] * 2,
        out_shape=[shape(keep_a.shape, jnp.int16)] * 2,
        compiler_params=params(),
        cost_estimate=cost(3),
        name="relayed_terms",
    )(keep_a, keep_b, near_y, near_x)


def neuron_kernel(
    own, near_y, near_x, late_a, late_b, theta, both, values, grads, hiddens, results, *, rate
):
    rows = own.shape[1]
    tokens = rows // STEPS
    half = rows // 2
    for i in range(own.shape[2] // LANES):
        columns = slice(i * LANES, (i + 1) * LANES)
        limit = theta[:, columns]
        for which, into in ((0, values), (1, grads)):
            for span, near, late in (
                (slice(0, half), near_y, late_a),
                (slice(half, rows), near_x, late_b),
            ):
                into[i, span] = own[which, span, columns] + (
                    decode(near[which, 0, :, columns], rate)
                    + decode(late[which, :, columns], rate)
                )
        membrane = jnp.zeros((tokens, LANES), jnp.float32)
        steps = []
        for step in range(STEPS):
            value = values[i, pl.ds(step, tokens, stride=STEPS), :]
            volt = membrane + value
            spike = jnp.clip((volt - limit) / spike_width + 0.5, 0.0, 1.0)
            membrane = volt - limit * spike
            hiddens[i, pl.ds(step, tokens, stride=STEPS), :] = spike * value
            steps.append((value, volt, spike))
        both[0, :, columns] = hiddens[i].astype(both.dtype)
        carry = jnp.zeros((tokens, LANES), jnp.float32)
        for step in range(STEPS - 1, -1, -1):
            value, volt, spike = steps[step]
            grad = grads[i, pl.ds(step, tokens, stride=STEPS), :]
            offset = 2.0 * (volt - limit) / spike_width
            gamma = 1.0 / (spike_width * (1.0 + offset * offset))
            dvolt = carry * (1.0 - limit * gamma) + grad * value * gamma
            results[i, pl.ds(step, tokens, stride=STEPS), :] = dvolt + grad * spike
            carry = dvolt
        both[1, :, columns] = results[i].astype(both.dtype)


def neurons(own, near_y, near_x, late_a, late_b, theta, rate):
    _, rows, quarter = own.shape
    return pl.pallas_call(
        functools.partial(neuron_kernel, rate=rate),
        in_specs=[VMEM] * 6,
        out_specs=VMEM,
        scratch_shapes=[pltpu.VMEM((quarter // LANES, rows, LANES), jnp.float32)] * 4,
        out_shape=shape((2, rows, quarter), jnp.bfloat16),
        compiler_params=params(),
        cost_estimate=cost(4),
        name="spiking_and_surrogate",
    )(own, near_y, near_x, late_a, late_b, theta)


def collect_kernel(*refs, count, carried, first_row):
    refs = list(refs)

    def take(count):
        taken, refs[:count] = refs[:count], []
        return taken

    lists = take(2)
    pieces = take(count)
    came_in = take(1)[0] if carried else None
    weights = take(2)
    _, out, whole_out = take(3)
    held = take(2)
    whole, came, part, acc, sems, in_sems, out_sems = refs
    _, rows, quarter = pieces[0].shape
    wide = acc.shape[1]
    width = min(BLOCK, quarter)
    parts = quarter // width
    moves = Copies(in_sems)
    leave = Copies(out_sems)
    if carried:
        moves.start(came_in, came)
    for r, source in enumerate(pieces[:3]):
        moves.start(source, whole.at[:, r])
    first = 0
    for source in pieces[3:]:
        moves.start(source, whole.at[:, 3, pl.ds(first, source.shape[1])])
        first += source.shape[1]

    def meanwhile():
        moves.finish()
        leave.start(whole, whole_out.at[:, :, pl.ds(first_row, rows), :])
        first = came.shape[1] if carried else 0
        for i in range(2):
            for j in range(wide):
                columns = slice(j * BLOCK, (j + 1) * BLOCK)
                if carried:
                    acc[i, j, :first] = came[i, :, columns].astype(jnp.float32)
                if first < rows:
                    acc[i, j, first:] = jnp.zeros((rows - first, BLOCK), jnp.float32)

    def use(i, g, k, block):
        r, piece = g // parts, g % parts
        columns = pl.ds(pl.multiple_of(piece * width, width), width)
        acc[i, k] += product(whole[i, r, :, columns], block[...], 1, i)

    each_kept(lists, weights, held, sems, width, (True, False), use, meanwhile)
    for i in range(2):
        for j in range(wide):
            part[i, :, j * BLOCK : (j + 1) * BLOCK] = acc[i, j].astype(part.dtype)
        leave.start(part.at[i], out.at[i])
    leave.finish()


def collect_terms(lists, pieces, came, w_up, w_down, out_type, earlier, first, all_rows):
    _, rows, quarter = pieces[0].shape
    features, units = w_up.shape
    _, width, _ = split_units(units)
    extra = [] if came is None else [came]
    came_dims = (2, 16, BLOCK) if came is None else came.shape
    whole_dims = (2, QUARTERS, rows, quarter)
    outs = [
        shape((2, rows, features), out_type),
        shape((2, QUARTERS, all_rows, quarter), pieces[0].dtype),
    ]
    if earlier is None:
        earlier, aliases = w_up, {}
    else:
        aliases = {4 + len(pieces) + len(extra): 1}
    return pl.pallas_call(
        functools.partial(
            collect_kernel, count=len(pieces), carried=came is not None, first_row=first
        ),
        in_specs=[SMEM] * 2 + [ANY] * (3 + len(pieces) + len(extra)),
        out_specs=[ANY] * len(outs),
        scratch_shapes=[
            pltpu.VMEM((SLOTS + 1, width, BLOCK), w_up.dtype),
            pltpu.VMEM((SLOTS + 1, BLOCK, width), w_up.dtype),
            pltpu.VMEM(whole_dims, pieces[0].dtype),
            pltpu.VMEM(came_dims, jnp.bfloat16),
            pltpu.VMEM((2, rows, features), out_type),
            pltpu.VMEM((2, features // BLOCK, rows, BLOCK), jnp.float32),
            pltpu.SemaphoreType.DMA((2, SLOTS)),
            pltpu.SemaphoreType.DMA((6,)),
            pltpu.SemaphoreType.DMA((3,)),
        ],
        out_shape=outs,
        input_output_aliases=aliases,
        compiler_params=params(),
        cost_estimate=cost(7),
        name="output_and_input_grad_terms",
    )(lists[1], lists[0], *pieces, *extra, w_down, w_up, earlier)


def clear_kernel(place, up, down, rows_up, rows_down, sems):
    rows_up[...] = jnp.zeros_like(rows_up)
    rows_down[...] = jnp.zeros_like(rows_down)
    copies = []
    for which, (whole, rows) in enumerate(((up, rows_up), (down, rows_down))):
        for i in range(PIECES):
            target = whole.at[pl.ds(i * rows.shape[0], rows.shape[0]), :]
            copies.append(pltpu.make_async_copy(rows, target, sems.at[which, i]))
    for copy in copies:
        copy.start()
    for copy in copies:
        copy.wait()


def cleared(place, features, units, kind):
    return pl.pallas_call(
        clear_kernel,
        in_specs=[SMEM],
        out_specs=[ANY, ANY],
        scratch_shapes=[
            pltpu.VMEM((features // PIECES, units), kind),
            pltpu.VMEM((units // PIECES, features), kind),
            pltpu.SemaphoreType.DMA((2, PIECES)),
        ],
        out_shape=[shape((features, units), kind), shape((units, features), kind)],
        compiler_params=params(),
        cost_estimate=cost(12),
        name="zero_weight_grads",
    )(place)


def weight_grads_kernel(*refs, places, count):
    lists = refs[:2]
    many = len(places)
    units = refs[2 : 2 + many]
    turned = refs[2 + many : 2 + many + count]
    outs = refs[4 + many + count : 6 + many + count]
    held_u, held_f, stage_up, stage_down, load_sems, out_sems = refs[6 + many + count :]
    width = stage_up.shape[2]
    parts = held_u.shape[3] // width
    stages = (stage_up, stage_down)

    def loads(which):
        pairs = []
        for source, first in zip(units, places):
            span = pl.ds(first, source.shape[2])
            pairs.append((source.at[1 - which], held_u.at[1 - which, :, span, :]))
        first = 0
        for source in turned:
            span = pl.ds(first, source.shape[2])
            first += source.shape[2]
            pairs.append((source.at[which], held_f.at[which, :, span]))
        return [
            pltpu.make_async_copy(source, target, load_sems.at[which, i])
            for i, (source, target) in enumerate(pairs)
        ]

    def store(which, n):
        entry = lists[which][n]
        slot = n % STAGES
        piece = pl.ds(pl.multiple_of((entry >> 16) * width, width), width)
        features = pl.ds(pl.multiple_of((entry & 255) * BLOCK, BLOCK), BLOCK)
        out = outs[which]
        target = out.at[piece, features] if which else out.at[features, piece]
        return pltpu.make_async_copy(stages[which].at[slot], target, out_sems.at[which, slot])

    first, second = loads(1), loads(0)
    for copy in first + second:
        copy.start()
    totals = [entries[entries.shape[0] - 1] for entries in lists]
    for which, copies in ((1, first), (0, second)):
        for copy in copies:
            copy.wait()

        def block(n, _, which=which):
            entry = lists[which][n]
            g = (entry >> 8) & 255
            features = pl.ds(pl.multiple_of((entry & 255) * BLOCK, BLOCK), BLOCK)
            columns = pl.ds(pl.multiple_of(g % parts * width, width), width)

            @pl.when(n >= STAGES)
            def _():
                store(which, n - STAGES).wait()

            value = product(
                held_f[which, features, :], held_u[1 - which, g // parts, :, columns], 1, 0
            )
            stage = stages[which]
            stage[n % STAGES] = (value.T if which else value).astype(stage.dtype)
            store(which, n).start()
            return 0

        lax.fori_loop(0, totals[which], block, 0)

    for which in (1, 0):

        def drain(n, _, which=which):
            store(which, n).wait()
            return 0

        lax.fori_loop(jnp.maximum(totals[which] - STAGES, 0), totals[which], drain, 0)


def weight_grads(lists, units, places, turned, zeros):
    count, many = len(turned), len(units)
    quarter = units[0].shape[-1]
    rows = sum(piece.shape[2] for piece in turned)
    features = turned[0].shape[1]
    width = min(BLOCK, quarter)
    kind = units[0].dtype
    return pl.pallas_call(
        functools.partial(weight_grads_kernel, places=places, count=count),
        in_specs=[SMEM] * 2 + [ANY] * (many + count + 2),
        out_specs=[ANY, ANY],
        scratch_shapes=[
            pltpu.VMEM((2, QUARTERS, rows, quarter), kind),
            pltpu.VMEM((2, features, rows), kind),
            pltpu.VMEM((STAGES, BLOCK, width), kind),
            pltpu.VMEM((STAGES, width, BLOCK), kind),
            pltpu.SemaphoreType.DMA((2, many + count)),
            pltpu.SemaphoreType.DMA((2, STAGES)),
        ],
        out_shape=[shape(zero.shape, kind) for zero in zeros],
        input_output_aliases={2 + many + count: 0, 3 + many + count: 1},
        compiler_params=params(),
        cost_estimate=cost(16),
        name="weight_grads",
    )(*lists, *units, *turned, *zeros)


def after(value, *others):
    return lax.optimization_barrier((value, *others))[0]


def across(value, flip):
    size = lax.axis_size("col")
    return lax.ppermute(value, "col", [(i, i ^ flip) for i in range(size)])


def other_core(value):
    return lax.ppermute(value, "dp", [(0, 1), (1, 0)])


def around(value):
    size = lax.axis_size("row")
    ring = list(range(0, size, 2)) + list(range(size - 1 - size % 2, 0, -2))
    return lax.ppermute(value, "row", [(ring[i], ring[(i + 1) % size]) for i in range(size)])


def per_device(inputs, w_up, mask_up, w_down, mask_down, threshold, cotangent):
    col_place = lax.axis_index("col").astype(jnp.int32)
    row_place = lax.axis_index("row").astype(jnp.int32)
    place = jnp.stack([col_place, row_place])
    features, units = w_up.shape
    quarter = units // QUARTERS
    rate = code_rate(features)
    theta = lax.dynamic_slice(threshold, (col_place * quarter,), (quarter,)).reshape(1, quarter)
    lists = kept_lists(place, mask_up, mask_down.T, features, units)
    rows = inputs.shape[0]

    ringed = lax.axis_size("row") == 4
    if ringed:
        rings = [(inputs, cotangent), around(jnp.stack([inputs, cotangent]))]
        count = 4
    else:
        both = jnp.stack([inputs, cotangent])
        rings = [lax.all_gather(both, "row", axis=1, tiled=True)]
        count = 1
        rows = rings[0].shape[1]

    terms, relays, gathered = ([None] * count for _ in range(3))
    lead = max(count - 1, 1)
    carry = dict.fromkeys(("mine", "came", "last", "zeros", "turned", "whole", "end"))

    def scatter(i):
        chunk = rings[i]
        if carry["last"] is not None:
            chunk = after(chunk, carry["last"])
        own, keep_a, keep_b, send_y, send_x, carry["turned"] = scatter_terms(
            lists, chunk, w_up, w_down, carry["turned"], i * rows, count * rows
        )
        terms[i] = (own, keep_a, keep_b, across(send_y, 2), across(send_x, 1))
        carry["last"] = own

    def hop():
        rings.append(around(after(rings[-1], carry["last"])))

    def clear():
        zeros = cleared(after(place, carry["last"]), features, units, w_up.dtype)
        carry["zeros"] = zeros
        carry["last"] = zeros[0]

    def pass_on(i):
        _, keep_a, keep_b, near_y, near_x = terms[i]
        keep_a = after(keep_a, carry["last"])
        late_a, late_b = relay(keep_a, keep_b, near_y, near_x, rate)
        relays[i] = (across(late_a, 1), across(late_b, 2))
        carry["last"] = late_a

    def fire(i):
        own, _, _, near_y, near_x = terms[i]
        pair = neurons(after(own, carry["last"]), near_y, near_x, *relays[i], theta, rate)
        over_x, over_y = across(pair, 1), across(pair, 2)
        if i == count - 1:
            carry["last"] = pair
            clear()
            over_x, over_y = after((over_x, over_y), carry["zeros"][0])
        if i in RELAYS:
            far = [across(over_y, 1) if RELAYS[i] == 1 else across(over_x, 2)]
        else:
            half = pair.shape[1] // 2
            far = [across(over_y[:, :half], 1), across(over_x[:, half:], 2)]
        gathered[i] = (pair, over_x, over_y, *far)
        if i < count - 1:
            carry["last"] = pair

    def collect(i):
        first = carry["mine"] is None
        kind = jnp.float32 if first else jnp.bfloat16
        pair, *others = gathered[i]
        end = i == lead
        part, whole = collect_terms(
            lists,
            (after(pair, carry["last"]), *others),
            carry["came"],
            w_up,
            w_down,
            kind,
            None if end else carry["whole"],
            0 if end else i * rows,
            rows if end else lead * rows,
        )
        if first:
            carry["mine"] = part
        else:
            carry["came"] = around(part)
        carry["end" if end else "whole"] = whole
        carry["last"] = part

    if ringed:
        order = ("S0", "H", "R0", "S1", "H", "F0", "S2", "R1", "F1", "C0", "R2", "S3", "F2", "C1")
        order += ("R3", "C2", "F3", "C3")
    else:
        order = ("S0", "R0", "F0", "C0")
    actions = {"S": scatter, "R": pass_on, "F": fire, "C": collect}
    for word in order:
        if word == "H":
            hop()
        else:
            actions[word[0]](int(word[1]))

    units = [carry["whole"]] + ([carry["end"]] if count > 1 else [])
    units += [other_core(value) for value in units]
    turned = [carry["turned"], other_core(carry["turned"])]
    places, first = [], 0
    for value in units:
        places.append(first)
        first += value.shape[2]
    up_grad, down_grad = weight_grads(lists, units, places, turned, carry["zeros"])
    mine, came = after(carry["mine"], up_grad), carry["came"]
    if ringed:
        ends = [mine[kind] + came[kind].astype(jnp.float32) for kind in range(2)]
    else:
        ends = lax.psum_scatter(mine, "row", scatter_dimension=1, tiled=True)
    output, input_grad = ends[0].astype(jnp.bfloat16), ends[1].astype(jnp.bfloat16)
    return (output, input_grad, up_grad, down_grad)


def solution(mesh):
    in_specs = (
        P(("dp", "row"), "col"),
        P("col", "row"),
        P(),
        P("row", "col"),
        P(),
        P("row"),
        P(("dp", "row"), "col"),
    )
    out_specs = (P(("dp", "row"), "col"), P(("dp", "row"), "col"), P("col", "row"), P("row", "col"))
    return jax.shard_map(
        per_device, mesh=mesh, in_specs=in_specs, out_specs=out_specs, check_vma=False
    )
```
